32 devices in a mesh: frame: 16 (over z, y, core), pos: 2 (over x).
Axes of the slice: x: 2, y: 2, z: 4, core: 2. Of those that a mesh axis runs over, the one named last changes fastest.
Arguments:
- spatial_qkv: bfloat16 [2, 16, 384, 3, 1152], P(None, 'frame', 'pos'), may hold values from -9 to 9
- residual: bfloat16 [2, 16, 384, 1152], P(None, 'frame', 'pos'), may hold values from -0.59765625 to 0.59765625
- spatial_gate: float32 [2, 1152], replicated, may hold values from 0.5 to 2
- spatial_proj: bfloat16 [1152, 1152], replicated, may hold values from -0.1875 to 0.1875
- spatial_qgain: float32 [72], replicated, may hold values from 0.5 to 8
- spatial_kgain: float32 [72], replicated, may hold values from 0.5 to 8
- temporal_shift: float32 [2, 1152], replicated, may hold values from -3 to 3
- temporal_scale: float32 [2, 1152], replicated, may hold values from -0.5 to 0.5
- temporal_qkv: bfloat16 [1152, 3456], replicated, as said below
- temporal_qgain: float32 [72], replicated, may hold values from 0.6 to 6
- temporal_kgain: float32 [72], replicated, may hold values from 0.6 to 6
Outputs:
- temporal_out: bfloat16 [2, 16, 384, 1152], P(None, 'frame', 'pos')
The draws below stay inside these ranges and needn't reach their ends.
Inputs may be any that keep to these rules, and one draw needn't show every extreme that they name: `temporal_qkv`: entries are of the size of a weight with fan-in 1152.
All inputs are finite; a program needn't handle non-finite values.
Results may differ from the reference program's by a relative error of at most 0.028.
The reference program's roundings to bfloat16 on the way count: a program that leaves them out, or rounds other values in their place, can miss the bound.
Values may be sent and summed in bfloat16 or wider, within the bound.
No kernel may reach another device: no remote copies, remote signals or barrier semaphores. Data moves between devices by JAX's collectives and lax.ppermute only.
A program may use at most 128 MiB of HBM per device.

```python
import math
import jax
import jax.numpy as jnp
from jax import lax

HEADS = 16
HEAD_DIM = 72
D = 1152
VIDEOS = 2
FRAMES = 16
POSITIONS = 384


def gain_pair(key, stream):
    key_query, key_keys = jax.random.split(jax.random.fold_in(key, stream))
    query_gain = jax.random.uniform(key_query, (HEAD_DIM,), jnp.float32, 0.6, 1.6)
    keys_gain = jax.random.uniform(key_keys, (HEAD_DIM,), jnp.float32, 0.6, 1.6)
    return (query_gain, keys_gain)


def draw_spatial_qgain(key, part):
    return gain_pair(key, 101)[0]


def draw_spatial_kgain(key, part):
    return gain_pair(key, 101)[1]


def draw_temporal_qgain(key, part):
    return gain_pair(key, 202)[0]


def draw_temporal_kgain(key, part):
    return gain_pair(key, 202)[1]


def draw_spatial_qkv(key, part):
    key_base = jax.random.fold_in(jax.random.fold_in(key, 303), 0)
    full_shape = (VIDEOS, FRAMES, POSITIONS, 3, HEADS, HEAD_DIM)
    values = jnp.clip(jax.random.normal(key_base, full_shape, jnp.float32), -6.0, 6.0)
    return values.reshape(VIDEOS, FRAMES, POSITIONS, 3, D).astype(jnp.bfloat16)


def draw_temporal_qkv(key, part):
    key_base = jax.random.fold_in(jax.random.fold_in(key, 404), 0)
    weights = jnp.clip(jax.random.normal(key_base, (D, 3, HEADS, HEAD_DIM), jnp.float32), -4.0, 4.0) / math.sqrt(D)
    return weights.reshape(D, 3 * D).astype(jnp.bfloat16)


def levels(stream_key, extent, pieces, low, high):
    level = 1.0
    for dim, shards_of in pieces:
        heights = jax.random.uniform(jax.random.fold_in(jax.random.fold_in(stream_key, 6), dim), (shards_of,), jnp.float32, low / len(pieces), high / len(pieces))
        level = level * jnp.repeat(jnp.exp(heights), extent[dim] // shards_of).reshape((-1,) + (1,) * (len(extent) - 1 - dim))
    return level


def scatter_about(own_key, extent, width, most, pieces=(), held_as=jnp.bfloat16):
    drawn = jax.random.normal(own_key, extent, jnp.float32) * width
    if len(pieces) > 0:
        drawn = levels(own_key, extent, pieces, -0.22, 0.18) * drawn
    return jnp.clip(drawn, min=-most, max=most).astype(held_as)


def setup_inputs(seed: int = 0) -> dict:
    key_list = jax.random.split(jax.random.key(seed), 12)
    spatial_qkv = draw_spatial_qkv(jax.random.fold_in(key_list[11], 71), 0)
    residual = scatter_about(key_list[1], (VIDEOS, FRAMES, POSITIONS, D), 0.1, 0.59765625, ((1, 16), (2, 2)))
    spatial_gate = jnp.clip(jax.random.uniform(key_list[2], (VIDEOS, D), jnp.float32, 0.5, 2.0), 0.5, 2.0)
    spatial_proj = scatter_about(key_list[3], (D, D), D ** -0.5, 0.1875)
    spatial_qgain = draw_spatial_qgain(jax.random.fold_in(key_list[11], 71), 0)
    spatial_kgain = draw_spatial_kgain(jax.random.fold_in(key_list[11], 71), 0)
    temporal_shift = scatter_about(key_list[6], (VIDEOS, D), 0.5, 3.0, (), jnp.float32)
    temporal_scale = jnp.clip(jax.random.uniform(key_list[7], (VIDEOS, D), jnp.float32, -0.5, 0.5), -0.5, 0.5)
    temporal_qkv = draw_temporal_qkv(jax.random.fold_in(key_list[11], 71), 0)
    temporal_qgain = draw_temporal_qgain(jax.random.fold_in(key_list[11], 71), 0)
    temporal_kgain = draw_temporal_kgain(jax.random.fold_in(key_list[11], 71), 0)
    return {"spatial_qkv": spatial_qkv, "residual": residual, "spatial_gate": spatial_gate, "spatial_proj": spatial_proj, "spatial_qgain": spatial_qgain, "spatial_kgain": spatial_kgain, "temporal_shift": temporal_shift, "temporal_scale": temporal_scale, "temporal_qkv": temporal_qkv, "temporal_qgain": temporal_qgain, "temporal_kgain": temporal_kgain}


EPSILON = 1e-06

def head_norm(values, gain):
    widened = values.astype(jnp.float32)
    factor = lax.rsqrt(lax.optimization_barrier(jnp.mean(widened * widened, axis=-1, keepdims=True)) + EPSILON)
    return (widened * factor * gain).astype(jnp.bfloat16)

def softmax_weights(scores):
    row_top = lax.optimization_barrier(jnp.max(scores, axis=-1, keepdims=True))
    expons = jnp.exp(scores - row_top)
    return (expons / lax.optimization_barrier(jnp.sum(expons, axis=-1, keepdims=True))).astype(jnp.bfloat16)

def spatial_attend(element, query_gain, keys_gain):
    query_norm = head_norm(element[:, 0], query_gain)
    keys_norm = head_norm(element[:, 1], keys_gain)
    scores = jnp.einsum('qhd,khd->hqk', query_norm.astype(jnp.float32), keys_norm.astype(jnp.float32)) / math.sqrt(HEAD_DIM)
    weights = softmax_weights(scores)
    return jnp.einsum('hqk,khd->qhd', weights.astype(jnp.float32), element[:, 2].astype(jnp.float32)).astype(jnp.bfloat16)

def modulate(updated, shift_rows, scale_rows):
    widened = updated.astype(jnp.float32)
    centred = widened - lax.optimization_barrier(jnp.mean(widened, axis=-1, keepdims=True))
    spread = lax.optimization_barrier(jnp.mean(centred * centred, axis=-1, keepdims=True))
    scaled = centred * lax.rsqrt(spread + EPSILON) * (1.0 + scale_rows[:, None, None, :])
    return (scaled + shift_rows[:, None, None, :]).astype(jnp.bfloat16)

def temporal_attend(projected, query_gain, keys_gain):
    query_norm = head_norm(projected[:, :, :, 0], query_gain)
    keys_norm = head_norm(projected[:, :, :, 1], keys_gain)
    scores = jnp.einsum('bfphd,bgphd->bphfg', query_norm.astype(jnp.float32), keys_norm.astype(jnp.float32)) / math.sqrt(HEAD_DIM)
    weights = softmax_weights(scores)
    result = jnp.einsum('bphfg,bgphd->bfphd', weights.astype(jnp.float32), projected[:, :, :, 2].astype(jnp.float32))
    return result.astype(jnp.bfloat16).reshape(VIDEOS, FRAMES, POSITIONS, D)

def reference(spatial_qkv, residual, spatial_gate, spatial_proj, spatial_qgain, spatial_kgain, temporal_shift, temporal_scale, temporal_qkv, temporal_qgain, temporal_kgain):
    stacked = spatial_qkv.reshape(VIDEOS * FRAMES, POSITIONS, 3, HEADS, HEAD_DIM)
    attended = lax.map(lambda element: spatial_attend(element, spatial_qgain, spatial_kgain), stacked)
    mixed = jnp.dot(attended.reshape(VIDEOS * FRAMES * POSITIONS, D), spatial_proj, preferred_element_type=jnp.float32)
    mixed = mixed.reshape(VIDEOS, FRAMES, POSITIONS, D)
    updated = (residual.astype(jnp.float32) + spatial_gate[:, None, None, :] * mixed).astype(jnp.bfloat16)
    normed = modulate(updated, temporal_shift, temporal_scale)
    projected = jnp.dot(normed.reshape(VIDEOS * FRAMES * POSITIONS, D), temporal_qkv, preferred_element_type=jnp.float32)
    projected = projected.astype(jnp.bfloat16).reshape(VIDEOS, FRAMES, POSITIONS, 3, HEADS, HEAD_DIM)
    return temporal_attend(projected, temporal_qgain, temporal_kgain)
```

```python
import functools
import math

import jax
import jax.numpy as jnp
from jax import lax
from jax.experimental import pallas as pl
from jax.experimental.pallas import tpu as pltpu
from jax.sharding import PartitionSpec as P

EPSILON = 1e-06
LANES = 128
F32 = jnp.float32
BF16 = jnp.bfloat16


def segment_masks(width, head_dim):
    feature = lax.broadcasted_iota(jnp.int32, (width, LANES), 0)
    head = lax.broadcasted_iota(jnp.int32, (width, LANES), 1)
    inside = feature - head * head_dim
    gather = jnp.where((inside >= 0) & (inside < head_dim), 1.0, 0.0).astype(BF16)
    feature = lax.broadcasted_iota(jnp.int32, (LANES, width), 1)
    head = lax.broadcasted_iota(jnp.int32, (LANES, width), 0)
    inside = feature - head * head_dim
    spread = jnp.where((inside >= 0) & (inside < head_dim), 1.0, 0.0).astype(BF16)
    return gather, spread


def split_dot(values, matrix):
    high = values.astype(BF16)
    low = (values - high.astype(F32)).astype(BF16)
    return jnp.dot(high, matrix, preferred_element_type=F32) + jnp.dot(
        low, matrix, preferred_element_type=F32
    )


def head_norm(values, gain_row, gather, spread, head_dim):
    widened = values.astype(F32)
    squares = split_dot(widened * widened, gather)
    factor = lax.rsqrt(squares * (1.0 / head_dim) + EPSILON)
    return (widened * split_dot(factor, spread) * gain_row).astype(BF16)


def head_window(head, head_dim, width):
    tiles = width // LANES
    start = LANES * min(head * head_dim // LANES, max(tiles - 2, 0))
    span = min(2 * LANES, width)
    lane = lax.broadcasted_iota(jnp.int32, (1, span), 1) + start
    mask = (lane >= head * head_dim) & (lane < (head + 1) * head_dim)
    return start, span, mask


def softmax_rows(scores, scale):
    top = jnp.max(scores, axis=-1, keepdims=True)
    expons = jnp.exp2((scores - top) * scale)
    total = jnp.sum(expons, axis=-1, keepdims=True)
    return (expons * (1.0 / total)).astype(BF16)


def spatial_kernel(head_dim, remotes, *refs):
    qkv_ref = refs[0]
    remote_refs = refs[1 : 1 + remotes]
    residual_ref, proj_ref, rows_ref, gains_ref, out_ref, keys, values, attended = refs[1 + remotes :]
    pos_loc, width = out_ref.shape
    heads = width // head_dim
    scale = math.log2(math.e) / math.sqrt(head_dim)
    gather, spread = segment_masks(width, head_dim)
    query = head_norm(qkv_ref[0, 0], gains_ref[0:1, :], gather, spread, head_dim)
    key_gain = gains_ref[1:2, :]
    keys[0:pos_loc, :] = head_norm(qkv_ref[0, 1], key_gain, gather, spread, head_dim)
    values[0:pos_loc, :] = qkv_ref[0, 2]
    for j, remote in enumerate(remote_refs):
        place = slice((j + 1) * pos_loc, (j + 2) * pos_loc)
        keys[place, :] = head_norm(remote[0], key_gain, gather, spread, head_dim)
        values[place, :] = remote[1]
    for head in range(heads):
        start, span, mask = head_window(head, head_dim, width)
        window = slice(start, start + span)
        own = jnp.where(mask, query[:, window], jnp.zeros((), BF16))
        scores = lax.dot_general(
            own, keys[:, window], (((1,), (1,)), ((), ())), preferred_element_type=F32
        )
        weights = softmax_rows(scores, scale)
        part = jnp.dot(weights, values[:, window], preferred_element_type=F32)
        attended[:, window] = jnp.where(mask, part, attended[:, window])
    mixed = jnp.dot(attended[...].astype(BF16), proj_ref[...], preferred_element_type=F32)
    updated = (residual_ref[0].astype(F32) + rows_ref[0, 0:1, :] * mixed).astype(BF16)
    widened = updated.astype(F32)
    centred = widened - jnp.mean(widened, axis=-1, keepdims=True)
    spread_of = jnp.mean(centred * centred, axis=-1, keepdims=True)
    scaled = centred * lax.rsqrt(spread_of + EPSILON) * (1.0 + rows_ref[0, 1:2, :])
    out_ref[...] = (scaled + rows_ref[0, 2:3, :]).astype(BF16)


def spatial(video, head_dim, qkv, remotes, residual, proj, rows, gains):
    _, _, pos_loc, width = qkv.shape
    all_pos = pos_loc * (1 + len(remotes))
    whole = lambda a: pl.BlockSpec(a.shape, lambda i: (0,) * a.ndim)
    return pl.pallas_call(
        functools.partial(spatial_kernel, head_dim, len(remotes)),
        grid=(1,),
        out_shape=jax.ShapeDtypeStruct((pos_loc, width), BF16),
        in_specs=[pl.BlockSpec((1, 3, pos_loc, width), lambda i: (video, 0, 0, 0))]
        + [whole(r) for r in remotes]
        + [
            pl.BlockSpec((1, pos_loc, width), lambda i: (video, 0, 0)),
            whole(proj),
            pl.BlockSpec((1, 3, width), lambda i: (video, 0, 0)),
            whole(gains),
        ],
        out_specs=pl.BlockSpec((pos_loc, width), lambda i: (0, 0)),
        scratch_shapes=[
            pltpu.VMEM((all_pos, width), BF16),
            pltpu.VMEM((all_pos, width), BF16),
            pltpu.VMEM((pos_loc, width), F32),
        ],
        compiler_params=pltpu.CompilerParams(vmem_limit_bytes=40 * 2**20),
        cost_estimate=pl.CostEstimate(
            flops=4 * pos_loc * all_pos * width + 2 * pos_loc * width * width,
            bytes_accessed=2 * width * (8 * pos_loc + width),
            transcendentals=0,
        ),
        name=f"spatial_{video}",
    )(qkv, *remotes, residual, proj, rows, gains)


def temporal_kernel(head_dim, block_tokens, in_ref, weight_ref, gains_ref, out_ref, arranged, query, keys, values, attended):
    frames, tokens, width = in_ref.shape
    heads = width // head_dim
    rows = frames * block_tokens
    blocks = tokens // block_tokens
    scale = math.log2(math.e) / math.sqrt(head_dim)
    gather, spread = segment_masks(width, head_dim)
    incoming = in_ref[...].astype(F32)
    for b in range(blocks):
        piece = incoming[:, b * block_tokens : (b + 1) * block_tokens, :]
        arranged[b * rows : (b + 1) * rows, :] = piece.reshape(rows, width).astype(BF16)
    for i, (place, gain) in enumerate(((query, 0), (keys, 1), (values, None))):
        projected = jnp.dot(
            arranged[...], weight_ref[:, i * width : (i + 1) * width], preferred_element_type=F32
        ).astype(BF16)
        if gain is not None:
            projected = head_norm(projected, gains_ref[gain : gain + 1, :], gather, spread, head_dim)
        place[...] = projected
    first = lax.broadcasted_iota(jnp.int32, (rows, rows), 0)
    second = lax.broadcasted_iota(jnp.int32, (rows, rows), 1)
    same = lax.rem(first, block_tokens) == lax.rem(second, block_tokens)
    for b in range(blocks):
        place = slice(b * rows, (b + 1) * rows)
        for head in range(heads):
            start, span, mask = head_window(head, head_dim, width)
            window = slice(start, start + span)
            own = jnp.where(mask, query[place, window], jnp.zeros((), BF16))
            scores = lax.dot_general(
                own, keys[place, window], (((1,), (1,)), ((), ())), preferred_element_type=F32
            )
            weights = softmax_rows(jnp.where(same, scores, -1e30), scale)
            part = jnp.dot(weights, values[place, window], preferred_element_type=F32)
            attended[place, window] = jnp.where(mask, part, attended[place, window])
    pieces = [
        attended[b * rows : (b + 1) * rows, :].reshape(frames, block_tokens, width)
        for b in range(blocks)
    ]
    out_ref[...] = jnp.concatenate(pieces, axis=1).astype(BF16)


def temporal(head_dim, moved, weight, gains):
    frames, tokens, width = moved.shape
    block_tokens = 8 if tokens % 8 == 0 else tokens
    total = frames * tokens
    whole = lambda a: pl.BlockSpec(a.shape, lambda i: (0,) * a.ndim)
    return pl.pallas_call(
        functools.partial(temporal_kernel, head_dim, block_tokens),
        grid=(1,),
        out_shape=jax.ShapeDtypeStruct(moved.shape, BF16),
        in_specs=[whole(moved), whole(weight), whole(gains)],
        out_specs=whole(moved),
        scratch_shapes=[pltpu.VMEM((total, width), BF16)] * 4 + [pltpu.VMEM((total, width), F32)],
        compiler_params=pltpu.CompilerParams(vmem_limit_bytes=44 * 2**20),
        cost_estimate=pl.CostEstimate(
            flops=2 * total * width * 3 * width, bytes_accessed=2 * width * (3 * width + 2 * total), transcendentals=0
        ),
        name="temporal",
    )(moved, weight, gains)


def per_device(
    spatial_qkv,
    residual,
    spatial_gate,
    spatial_proj,
    spatial_qgain,
    spatial_kgain,
    temporal_shift,
    temporal_scale,
    temporal_qkv,
    temporal_qgain,
    temporal_kgain,
):
    videos, frames_loc, pos_loc, _, width = spatial_qkv.shape
    head_dim = spatial_qgain.shape[0]
    heads = width // head_dim
    pos_count = lax.axis_size("pos")
    frame_count = lax.axis_size("frame")
    assert frames_loc == 1
    qkv = jnp.transpose(spatial_qkv.reshape(videos, pos_loc, 3, width), (0, 2, 1, 3))
    residual = residual.reshape(videos, pos_loc, width)
    remotes = []
    for video in range(videos):
        own = qkv[video, 1:]
        remotes.append(
            [
                lax.ppermute(own, "pos", [(i, (i + s) % pos_count) for i in range(pos_count)])
                for s in range(1, pos_count)
            ]
        )
    rows = jnp.stack([spatial_gate, temporal_scale, temporal_shift], axis=1)
    tile = lambda a, b: jnp.tile(jnp.stack([a, b]), (1, heads))
    spatial_gains = tile(spatial_qgain, spatial_kgain)
    temporal_gains = tile(temporal_qgain, temporal_kgain)
    normed = [
        spatial(video, head_dim, qkv, remotes[video], residual, spatial_proj, rows, spatial_gains)
        for video in range(videos)
    ]
    tokens = videos * pos_loc // frame_count
    outgoing = jnp.concatenate(normed, axis=0).reshape(frame_count, tokens, width)
    moved = lax.all_to_all(outgoing, "frame", split_axis=0, concat_axis=0, tiled=True)
    result = temporal(head_dim, moved, temporal_qkv, temporal_gains)
    back = lax.all_to_all(result, "frame", split_axis=0, concat_axis=0, tiled=True)
    return back.reshape(videos, frames_loc, pos_loc, width)


def solution(mesh):
    return jax.shard_map(
        per_device,
        mesh=mesh,
        in_specs=(
            P(None, "frame", "pos", None, None),
            P(None, "frame", "pos", None),
            P(),
            P(),
            P(),
            P(),
            P(),
            P(),
            P(),
            P(),
            P(),
        ),
        out_specs=P(None, "frame", "pos", None),
        check_vma=False,
    )
```

```python
import functools
import math

import jax
import jax.numpy as jnp
from jax import lax
from jax.experimental import pallas as pl
from jax.experimental.pallas import tpu as pltpu
from jax.sharding import PartitionSpec as P

EPSILON = 1e-06
LANES = 128
F32 = jnp.float32
BF16 = jnp.bfloat16
VMEM_LIMIT = 24 * 2**20
TEMPORAL_LIMIT = 57 * 2**20
SMALL, LARGE = 5 * 10**8, 2 * 10**10


def segment_masks(width, head_dim):
    feature = lax.broadcasted_iota(jnp.int32, (width, LANES), 0)
    head = lax.broadcasted_iota(jnp.int32, (width, LANES), 1)
    inside = feature - head * head_dim
    gather = jnp.where((inside >= 0) & (inside < head_dim), 1.0, 0.0).astype(BF16)
    feature = lax.broadcasted_iota(jnp.int32, (LANES, width), 1)
    head = lax.broadcasted_iota(jnp.int32, (LANES, width), 0)
    inside = feature - head * head_dim
    spread = jnp.where((inside >= 0) & (inside < head_dim), 1.0, 0.0).astype(BF16)
    return gather, spread


def split_dot(values, matrix):
    high = values.astype(BF16)
    low = (values - high.astype(F32)).astype(BF16)
    return jnp.dot(high, matrix, preferred_element_type=F32) + jnp.dot(
        low, matrix, preferred_element_type=F32
    )


def head_norm(values, gain_row, gather, spread, head_dim):
    widened = values.astype(F32)
    squares = split_dot(widened * widened, gather)
    factor = lax.rsqrt(squares * (1.0 / head_dim) + EPSILON)
    return (widened * split_dot(factor, spread) * gain_row).astype(BF16)


def head_window(head, head_dim, width):
    tiles = width // LANES
    start = LANES * min(head * head_dim // LANES, max(tiles - 2, 0))
    span = min(2 * LANES, width)
    lane = lax.broadcasted_iota(jnp.int32, (1, span), 1) + start
    mask = (lane >= head * head_dim) & (lane < (head + 1) * head_dim)
    return start, span, mask


def softmax_rows(scores, scale):
    top = jnp.max(scores, axis=-1, keepdims=True)
    expons = jnp.exp2((scores - top) * scale)
    total = jnp.sum(expons, axis=-1, keepdims=True)
    return (expons * (1.0 / total)).astype(BF16)


def score_kernel(head_dim, video, remotes, *refs):
    qkv_ref = refs[0]
    remote_refs = refs[1 : 1 + remotes]
    gains_ref, out_ref, query, keys = refs[1 + remotes :]
    pos_loc, width = query.shape
    scale = math.log2(math.e) / math.sqrt(head_dim)
    gather, spread = segment_masks(width, head_dim)
    query[...] = head_norm(qkv_ref[video, 0], gains_ref[0:1, :], gather, spread, head_dim)
    key_gain = gains_ref[1:2, :]
    keys[0:pos_loc, :] = head_norm(qkv_ref[video, 1], key_gain, gather, spread, head_dim)
    for j, remote in enumerate(remote_refs):
        place = slice((j + 1) * pos_loc, (j + 2) * pos_loc)
        keys[place, :] = head_norm(remote[...], key_gain, gather, spread, head_dim)
    for head in range(width // head_dim):
        start, span, mask = head_window(head, head_dim, width)
        window = slice(start, start + span)
        own = jnp.where(mask, query[:, window], jnp.zeros((), BF16))
        scores = lax.dot_general(
            own, keys[:, window], (((1,), (1,)), ((), ())), preferred_element_type=F32
        )
        out_ref[head] = softmax_rows(scores, scale)


def in_vmem(count):
    return [pl.BlockSpec(memory_space=pltpu.VMEM)] * count


def score_weights(video, head_dim, qkv, remote_keys, gains):
    _, _, pos_loc, width = qkv.shape
    all_pos = pos_loc * (1 + len(remote_keys))
    heads = width // head_dim
    return pl.pallas_call(
        functools.partial(score_kernel, head_dim, video, len(remote_keys)),
        out_shape=jax.ShapeDtypeStruct((heads, pos_loc, all_pos), BF16),
        in_specs=in_vmem(2 + len(remote_keys)),
        out_specs=pl.BlockSpec(memory_space=pltpu.VMEM),
        scratch_shapes=[pltpu.VMEM((pos_loc, width), BF16), pltpu.VMEM((all_pos, width), BF16)],
        compiler_params=pltpu.CompilerParams(vmem_limit_bytes=VMEM_LIMIT),
        cost_estimate=pl.CostEstimate(flops=SMALL, bytes_accessed=2**20, transcendentals=0),
        name=f"scores_{video}",
    )(qkv, *remote_keys, gains)


def attend_kernel(head_dim, video, remotes, sub, *refs):
    weights_ref, qkv_ref = refs[:2]
    remote_refs = refs[2 : 2 + remotes]
    residual_ref, proj_ref, gate_ref, scale_ref, shift_ref, out_ref, values, attended = refs[2 + remotes :]
    pos_loc, width = attended.shape
    row = slice(video, video + 1)
    values[0:pos_loc, :] = qkv_ref[video, 2]
    for j, remote in enumerate(remote_refs):
        values[(j + 1) * pos_loc : (j + 2) * pos_loc, :] = remote[...]
    for head in range(width // head_dim):
        start, span, mask = head_window(head, head_dim, width)
        window = slice(start, start + span)
        part = jnp.dot(weights_ref[head], values[:, window], preferred_element_type=F32)
        attended[:, window] = jnp.where(mask, part, attended[:, window])
    mixed = jnp.dot(attended[...].astype(BF16), proj_ref[...], preferred_element_type=F32)
    updated = (residual_ref[video].astype(F32) + gate_ref[row, :] * mixed).astype(BF16)
    widened = updated.astype(F32)
    centred = widened - jnp.mean(widened, axis=-1, keepdims=True)
    spread_of = jnp.mean(centred * centred, axis=-1, keepdims=True)
    scaled = centred * lax.rsqrt(spread_of + EPSILON) * (1.0 + scale_ref[row, :])
    attended[...] = scaled + shift_ref[row, :]
    for i in range(pos_loc // sub):
        out_ref[i] = attended[i * sub : (i + 1) * sub, :].astype(BF16)


def attend(video, head_dim, sub, cost, weights, qkv, remote_values, residual, proj, gate, scale, shift):
    _, _, pos_loc, width = qkv.shape
    all_pos = pos_loc * (1 + len(remote_values))
    return pl.pallas_call(
        functools.partial(attend_kernel, head_dim, video, len(remote_values), sub),
        out_shape=jax.ShapeDtypeStruct((pos_loc // sub, sub, width), BF16),
        in_specs=in_vmem(7 + len(remote_values)),
        out_specs=pl.BlockSpec(memory_space=pltpu.VMEM),
        scratch_shapes=[pltpu.VMEM((all_pos, width), BF16), pltpu.VMEM((pos_loc, width), F32)],
        compiler_params=pltpu.CompilerParams(vmem_limit_bytes=VMEM_LIMIT),
        cost_estimate=pl.CostEstimate(flops=cost, bytes_accessed=2**20, transcendentals=0),
        name=f"attend_{video}",
    )(weights, qkv, *remote_values, residual, proj, gate, scale, shift)


def temporal_kernel(
    head_dim, tokens, in_ref, weight_ref, gains_ref, out_ref, arranged, query, keys, values, bias, held, arrived
):
    pieces, sub, width = in_ref.shape
    columns = [slice(i * width, (i + 1) * width) for i in range(3)]
    copies = [
        pltpu.make_async_copy(weight_ref.at[:, c], held.at[:, c], arrived.at[i])
        for i, c in enumerate(columns)
    ]
    for copy in copies:
        copy.start()
    rows = pieces * sub
    scale = math.log2(math.e) / math.sqrt(head_dim)
    gather, spread = segment_masks(width, head_dim)
    for i in range(pieces):
        arranged[i * sub : (i + 1) * sub, :] = in_ref[i].astype(F32)
    incoming = arranged[...].astype(BF16)
    for i, (place, gain) in enumerate(((query, 2), (keys, 3), (values, None))):
        copies[i].wait()
        projected = jnp.dot(
            incoming, held[:, columns[i]], preferred_element_type=F32
        ).astype(BF16)
        if gain is not None:
            projected = head_norm(projected, gains_ref[gain : gain + 1, :], gather, spread, head_dim)
        place[...] = projected
    first = lax.broadcasted_iota(jnp.int32, (rows, rows), 0)
    second = lax.broadcasted_iota(jnp.int32, (rows, rows), 1)
    same = lax.rem(first, tokens) == lax.rem(second, tokens)
    bias[...] = jnp.where(same, 0.0, -1e30)
    for head in range(width // head_dim):
        start, span, mask = head_window(head, head_dim, width)
        window = slice(start, start + span)
        own = jnp.where(mask, query[:, window], jnp.zeros((), BF16))
        scores = lax.dot_general(
            own, keys[:, window], (((1,), (1,)), ((), ())), preferred_element_type=F32
        )
        weights = softmax_rows(scores + bias[...], scale)
        part = jnp.dot(weights, values[:, window], preferred_element_type=F32)
        arranged[:, window] = jnp.where(mask, part, arranged[:, window])
    for i in range(pieces):
        out_ref[i] = arranged[i * sub : (i + 1) * sub, :].astype(BF16)


def temporal(video, head_dim, tokens, moved, weight, gains):
    pieces, sub, width = moved.shape
    rows = pieces * sub
    return pl.pallas_call(
        functools.partial(temporal_kernel, head_dim, tokens),
        out_shape=jax.ShapeDtypeStruct(moved.shape, BF16),
        in_specs=in_vmem(1) + [pl.BlockSpec(memory_space=pltpu.HBM)] + in_vmem(1),
        out_specs=pl.BlockSpec(memory_space=pltpu.VMEM),
        scratch_shapes=[pltpu.VMEM((rows, width), F32)]
        + [pltpu.VMEM((rows, width), BF16)] * 3
        + [
            pltpu.VMEM((rows, rows), F32),
            pltpu.VMEM((width, 3 * width), BF16),
            pltpu.SemaphoreType.DMA((3,)),
        ],
        compiler_params=pltpu.CompilerParams(vmem_limit_bytes=TEMPORAL_LIMIT),
        cost_estimate=pl.CostEstimate(flops=SMALL, bytes_accessed=2**20, transcendentals=0),
        name=f"temporal_{video}",
    )(moved, weight, gains)


def exchange(blocks, frame_count):
    pieces, sub, width = blocks.shape
    split = blocks.reshape(frame_count, pieces // frame_count, sub, width)
    moved = lax.all_to_all(split, "frame", split_axis=0, concat_axis=0, tiled=True)
    return moved.reshape(pieces, sub, width)


def per_device(
    spatial_qkv,
    residual,
    spatial_gate,
    spatial_proj,
    spatial_qgain,
    spatial_kgain,
    temporal_shift,
    temporal_scale,
    temporal_qkv,
    temporal_qgain,
    temporal_kgain,
):
    videos, frames_loc, pos_loc, _, width = spatial_qkv.shape
    head_dim = spatial_qgain.shape[0]
    heads = width // head_dim
    pos_count = lax.axis_size("pos")
    frame_count = lax.axis_size("frame")
    assert frames_loc == 1
    tokens = pos_loc // frame_count
    sub = math.gcd(tokens, 8)
    qkv = jnp.transpose(spatial_qkv.reshape(videos, pos_loc, 3, width), (0, 2, 1, 3))
    residual = residual.reshape(videos, pos_loc, width)
    steps = [[(i, (i + s) % pos_count) for i in range(pos_count)] for s in range(1, pos_count)]
    remotes = {}
    for video in reversed(range(videos)):
        for which in (2, 1):
            own = qkv[video, which]
            remotes[video, which] = [lax.ppermute(own, "pos", step) for step in steps]
    gains = jnp.tile(
        jnp.stack([spatial_qgain, spatial_kgain, temporal_qgain, temporal_kgain]), (1, heads)
    )
    results = []
    for video in range(videos):
        weights = score_weights(video, head_dim, qkv, remotes[video, 1], gains)
        normed = attend(
            video, head_dim, sub, LARGE if video == videos - 1 else SMALL, weights, qkv, remotes[video, 2], residual,
            spatial_proj, spatial_gate, temporal_scale, temporal_shift,
        )
        moved = exchange(normed, frame_count)
        result = temporal(video, head_dim, tokens, moved, temporal_qkv, gains)
        back = exchange(result, frame_count)
        results.append(back.reshape(pos_loc, width))
    return jnp.stack(results).reshape(videos, frames_loc, pos_loc, width)


def solution(mesh):
    return jax.shard_map(
        per_device,
        mesh=mesh,
        in_specs=(
            P(None, "frame", "pos", None, None),
            P(None, "frame", "pos", None),
            P(),
            P(),
            P(),
            P(),
            P(),
            P(),
            P(),
            P(),
            P(),
        ),
        out_specs=P(None, "frame", "pos", None),
        check_vma=False,
    )
```

```python
import functools
import math

import jax
import jax.numpy as jnp
from jax import lax
from jax.experimental import pallas as pl
from jax.experimental.pallas import tpu as pltpu
from jax.sharding import PartitionSpec as P

EPSILON = 1e-06
LANES = 128
F32 = jnp.float32
BF16 = jnp.bfloat16
TEMPORAL_LIMIT = 50 * 2**20
VMEM_LIMIT = 24 * 2**20
TLAST = 5 * 10**8
PLACE = 7 * 10**9
SHUFFLE_LIMIT = 8 * 2**20
SMALL, LARGE = 5 * 10**8, 2 * 10**10


def segment_masks(width, head_dim):
    feature = lax.broadcasted_iota(jnp.int32, (width, LANES), 0)
    head = lax.broadcasted_iota(jnp.int32, (width, LANES), 1)
    inside = feature - head * head_dim
    gather = jnp.where((inside >= 0) & (inside < head_dim), 1.0, 0.0).astype(BF16)
    feature = lax.broadcasted_iota(jnp.int32, (LANES, width), 1)
    head = lax.broadcasted_iota(jnp.int32, (LANES, width), 0)
    inside = feature - head * head_dim
    spread = jnp.where((inside >= 0) & (inside < head_dim), 1.0, 0.0).astype(BF16)
    return gather, spread


def split_dot(values, matrix):
    high = values.astype(BF16)
    low = (values - high.astype(F32)).astype(BF16)
    return jnp.dot(high, matrix, preferred_element_type=F32) + jnp.dot(
        low, matrix, preferred_element_type=F32
    )


def head_norm(values, gain_ref, gather, spread, head_dim):
    gain_row = jnp.concatenate([gain_ref[...]] * (values.shape[1] // head_dim), axis=1)
    widened = values.astype(F32)
    squares = split_dot(widened * widened, gather)
    factor = lax.rsqrt(squares * (1.0 / head_dim) + EPSILON)
    return (widened * split_dot(factor, spread) * gain_row).astype(BF16)


def head_window(head, head_dim, width):
    tiles = width // LANES
    start = LANES * min(head * head_dim // LANES, max(tiles - 2, 0))
    span = min(2 * LANES, width)
    lane = lax.broadcasted_iota(jnp.int32, (1, span), 1) + start
    mask = (lane >= head * head_dim) & (lane < (head + 1) * head_dim)
    return start, span, mask


def softmax_rows(scores, scale):
    top = jnp.max(scores, axis=-1, keepdims=True)
    expons = jnp.exp2((scores - top) * scale)
    total = jnp.sum(expons, axis=-1, keepdims=True)
    return (expons * (1.0 / total)).astype(BF16)


def score_kernel(head_dim, video, remotes, *refs):
    qkv_ref = refs[0]
    remote_refs = refs[1 : 1 + remotes]
    query_gain, key_gain, out_ref, query, keys = refs[1 + remotes :]
    pos_loc, width = query.shape
    scale = math.log2(math.e) / math.sqrt(head_dim)
    gather, spread = segment_masks(width, head_dim)
    query[...] = head_norm(qkv_ref[video, 0], query_gain, gather, spread, head_dim)
    keys[0:pos_loc, :] = head_norm(qkv_ref[video, 1], key_gain, gather, spread, head_dim)
    for j, remote in enumerate(remote_refs):
        place = slice((j + 1) * pos_loc, (j + 2) * pos_loc)
        keys[place, :] = head_norm(remote[...], key_gain, gather, spread, head_dim)
    for head in range(width // head_dim):
        start, span, mask = head_window(head, head_dim, width)
        window = slice(start, start + span)
        own = jnp.where(mask, query[:, window], jnp.zeros((), BF16))
        scores = lax.dot_general(
            own, keys[:, window], (((1,), (1,)), ((), ())), preferred_element_type=F32
        )
        out_ref[head] = softmax_rows(scores, scale)


def in_vmem(count):
    return [pl.BlockSpec(memory_space=pltpu.VMEM)] * count


def score_weights(video, head_dim, qkv, remote_keys, query_gain, key_gain):
    _, _, pos_loc, width = qkv.shape
    all_pos = pos_loc * (1 + len(remote_keys))
    heads = width // head_dim
    return pl.pallas_call(
        functools.partial(score_kernel, head_dim, video, len(remote_keys)),
        out_shape=jax.ShapeDtypeStruct((heads, pos_loc, all_pos), BF16),
        in_specs=in_vmem(3 + len(remote_keys)),
        out_specs=pl.BlockSpec(memory_space=pltpu.VMEM),
        scratch_shapes=[pltpu.VMEM((pos_loc, width), BF16), pltpu.VMEM((all_pos, width), BF16)],
        compiler_params=pltpu.CompilerParams(vmem_limit_bytes=VMEM_LIMIT),
        cost_estimate=pl.CostEstimate(flops=SMALL, bytes_accessed=2**20, transcendentals=0),
        name=f"scores_{video}",
    )(qkv, *remote_keys, query_gain, key_gain)


def attend_kernel(head_dim, video, remotes, sub, *refs):
    weights_ref, qkv_ref = refs[:2]
    remote_refs = refs[2 : 2 + remotes]
    residual_ref, proj_ref, gate_ref, scale_ref, shift_ref, out_ref, values, attended = refs[2 + remotes :]
    pos_loc, width = attended.shape
    row = slice(video, video + 1)
    values[0:pos_loc, :] = qkv_ref[video, 2]
    for j, remote in enumerate(remote_refs):
        values[(j + 1) * pos_loc : (j + 2) * pos_loc, :] = remote[...]
    for head in range(width // head_dim):
        start, span, mask = head_window(head, head_dim, width)
        window = slice(start, start + span)
        part = jnp.dot(weights_ref[head], values[:, window], preferred_element_type=F32)
        attended[:, window] = jnp.where(mask, part, attended[:, window])
    mixed = jnp.dot(attended[...].astype(BF16), proj_ref[...], preferred_element_type=F32)
    updated = (residual_ref[video].astype(F32) + gate_ref[row, :] * mixed).astype(BF16)
    widened = updated.astype(F32)
    centred = widened - jnp.mean(widened, axis=-1, keepdims=True)
    spread_of = jnp.mean(centred * centred, axis=-1, keepdims=True)
    scaled = centred * lax.rsqrt(spread_of + EPSILON) * (1.0 + scale_ref[row, :])
    attended[...] = scaled + shift_ref[row, :]
    for i in range(pos_loc // sub):
        out_ref[i] = attended[i * sub : (i + 1) * sub, :].astype(BF16)


def attend(video, head_dim, sub, cost, weights, qkv, remote_values, residual, proj, gate, scale, shift):
    _, _, pos_loc, width = qkv.shape
    all_pos = pos_loc * (1 + len(remote_values))
    return pl.pallas_call(
        functools.partial(attend_kernel, head_dim, video, len(remote_values), sub),
        out_shape=jax.ShapeDtypeStruct((pos_loc // sub, sub, width), BF16),
        in_specs=in_vmem(7 + len(remote_values)),
        out_specs=pl.BlockSpec(memory_space=pltpu.VMEM),
        scratch_shapes=[pltpu.VMEM((all_pos, width), BF16), pltpu.VMEM((pos_loc, width), F32)],
        compiler_params=pltpu.CompilerParams(vmem_limit_bytes=VMEM_LIMIT),
        cost_estimate=pl.CostEstimate(flops=cost, bytes_accessed=2**20, transcendentals=0),
        name=f"attend_{video}",
    )(weights, qkv, *remote_values, residual, proj, gate, scale, shift)


def temporal_kernel(head_dim, tokens, outer, *refs):
    me_ref, in_ref, weight_ref, query_gain, key_gain = refs[:5]
    arranged, query, keys, values, bias, total, held, arrived = refs[-8:]
    out_refs = refs[5:-8]
    pieces, sub, width = in_ref.shape
    cuts = [0, max(width // 4 // 256, 1) * 256, max(width // 2 // 256, 1) * 256, width]
    copies = [
        pltpu.make_async_copy(weight_ref.at[low:high], held.at[low:high], arrived.at[i])
        for i, (low, high) in enumerate(zip(cuts[:-1], cuts[1:]))
        if low < high
    ]
    for copy in copies:
        copy.start()
    rows = pieces * sub
    scale = math.log2(math.e) / math.sqrt(head_dim)
    gather, spread = segment_masks(width, head_dim)
    for i in range(pieces):
        arranged[i * sub : (i + 1) * sub, :] = in_ref[i].astype(F32)
    incoming = arranged[...].astype(BF16)
    half = cuts[2]
    columns = [slice(i * width, (i + 1) * width) for i in range(3)]
    for copy in copies[:-1]:
        copy.wait()
    for c in columns:
        total[:, c] = jnp.dot(incoming[:, :half], held[:half, c], preferred_element_type=F32)
    copies[-1].wait()
    for place, gain, c in ((query, query_gain, columns[0]), (keys, key_gain, columns[1]), (values, None, columns[2])):
        rest = jnp.dot(incoming[:, half:], held[half:, c], preferred_element_type=F32)
        projected = (total[:, c] + rest).astype(BF16)
        if gain is not None:
            projected = head_norm(projected, gain, gather, spread, head_dim)
        place[...] = projected
    first = lax.broadcasted_iota(jnp.int32, (rows, rows), 0)
    second = lax.broadcasted_iota(jnp.int32, (rows, rows), 1)
    same = lax.rem(first, tokens) == lax.rem(second, tokens)
    bias[...] = jnp.where(same, 0.0, -1e30)
    for head in range(width // head_dim):
        start, span, mask = head_window(head, head_dim, width)
        window = slice(start, start + span)
        own = jnp.where(mask, query[:, window], jnp.zeros((), BF16))
        scores = lax.dot_general(
            own, keys[:, window], (((1,), (1,)), ((), ())), preferred_element_type=F32
        )
        weights = softmax_rows(scores + bias[...], scale)
        part = jnp.dot(weights, values[:, window], preferred_element_type=F32)
        arranged[:, window] = jnp.where(mask, part, arranged[:, window])
    if outer == 1:
        for i in range(pieces):
            out_refs[0][i] = arranged[i * sub : (i + 1) * sub, :].astype(BF16)
        return
    share = rows // outer
    me = lax.div(me_ref[0], rows // tokens // outer)
    for s in range(outer):
        block = arranged[pl.ds(pl.multiple_of(send_to(me, s, outer) * share, sub), share), :]
        for i in range(share // sub):
            out_refs[s][i] = block[i * sub : (i + 1) * sub, :].astype(BF16)


def temporal(video, head_dim, tokens, outer, cost, me, moved, weight, gains):
    pieces, sub, width = moved.shape
    rows = pieces * sub
    return pl.pallas_call(
        functools.partial(temporal_kernel, head_dim, tokens, outer),
        out_shape=[jax.ShapeDtypeStruct((pieces // outer, sub, width), BF16)] * outer,
        in_specs=[pl.BlockSpec(memory_space=pltpu.SMEM)]
        + in_vmem(1)
        + [pl.BlockSpec(memory_space=pltpu.HBM)]
        + in_vmem(2),
        out_specs=in_vmem(outer),
        scratch_shapes=[pltpu.VMEM((rows, width), F32)]
        + [pltpu.VMEM((rows, width), BF16)] * 3
        + [
            pltpu.VMEM((rows, rows), F32),
            pltpu.VMEM((rows, 3 * width), F32),
            pltpu.VMEM((width, 3 * width), BF16),
            pltpu.SemaphoreType.DMA((3,)),
        ],
        compiler_params=pltpu.CompilerParams(vmem_limit_bytes=TEMPORAL_LIMIT),
        cost_estimate=pl.CostEstimate(flops=cost, bytes_accessed=2**20, transcendentals=0),
        name=f"temporal_{video}",
    )(me, moved, weight, *gains)


def send_to(me, step, count):
    return me ^ step if count & (count - 1) == 0 else lax.rem(me + step, count)


def come_from(me, step, count):
    return me ^ step if count & (count - 1) == 0 else lax.rem(me + count - step, count)


def partners(step, count):
    return [i ^ step if count & (count - 1) == 0 else (i + step) % count for i in range(count)]


def regroup_kernel(outer, inner, me_ref, *refs):
    share = refs[0].shape[0] // inner
    me = lax.rem(me_ref[0], inner)
    for t in range(inner):
        to = send_to(me, t, inner)
        for s in range(outer):
            refs[outer + t][s * share : (s + 1) * share] = refs[s][pl.ds(to * share, share)]


def place_kernel(outer, inner, me_ref, *refs):
    share = refs[0].shape[0] // outer
    me = me_ref[0]
    for t in range(inner):
        low = come_from(lax.rem(me, inner), t, inner)
        for s in range(outer):
            high = come_from(lax.div(me, inner), s, outer)
            refs[inner][pl.ds((high * inner + low) * share, share)] = refs[t][
                s * share : (s + 1) * share
            ]


def shuffle(kernel, name, cost, outer, inner, me, arrays, shapes):
    return pl.pallas_call(
        functools.partial(kernel, outer, inner),
        out_shape=[jax.ShapeDtypeStruct(shape, BF16) for shape in shapes],
        in_specs=[pl.BlockSpec(memory_space=pltpu.SMEM)] + in_vmem(len(arrays)),
        out_specs=in_vmem(len(shapes)),
        compiler_params=pltpu.CompilerParams(vmem_limit_bytes=SHUFFLE_LIMIT),
        cost_estimate=pl.CostEstimate(flops=cost, bytes_accessed=2**20, transcendentals=0),
        name=name,
    )(me, *arrays)


def way_back(blocks, me, outer, inner):
    pieces, sub, width = blocks[0].shape
    count = outer * inner
    held = [blocks[0]]
    for s in range(1, outer):
        to = partners(s, outer)
        pairs = [(i, to[i // inner] * inner + i % inner) for i in range(count)]
        held.append(lax.ppermute(blocks[s], "frame", pairs))
    share = pieces // inner
    grouped = shuffle(
        regroup_kernel, "regroup", 1000, outer, inner, me, held, [(outer * share, sub, width)] * inner
    )
    held = [grouped[0]]
    for t in range(1, inner):
        to = partners(t, inner)
        pairs = [(i, i // inner * inner + to[i % inner]) for i in range(count)]
        held.append(lax.ppermute(grouped[t], "frame", pairs))
    (placed,) = shuffle(
        place_kernel, "place", PLACE, outer, inner, me, held, [(count * share, sub, width)]
    )
    return placed


def exchange(blocks, frame_count):
    pieces, sub, width = blocks.shape
    split = blocks.reshape(frame_count, pieces // frame_count, sub, width)
    moved = lax.all_to_all(split, "frame", split_axis=0, concat_axis=0, tiled=True)
    return moved.reshape(pieces, sub, width)


def per_device(
    spatial_qkv,
    residual,
    spatial_gate,
    spatial_proj,
    spatial_qgain,
    spatial_kgain,
    temporal_shift,
    temporal_scale,
    temporal_qkv,
    temporal_qgain,
    temporal_kgain,
):
    videos, frames_loc, pos_loc, _, width = spatial_qkv.shape
    head_dim = spatial_qgain.shape[0]
    pos_count = lax.axis_size("pos")
    frame_count = lax.axis_size("frame")
    assert frames_loc == 1
    tokens = pos_loc // frame_count
    sub = math.gcd(tokens, 8)
    inner = math.gcd(frame_count, 4)
    outer = frame_count // inner
    me = lax.axis_index("frame").astype(jnp.int32).reshape(1)
    qkv = jnp.transpose(spatial_qkv.reshape(videos, pos_loc, 3, width), (0, 2, 1, 3))
    residual = residual.reshape(videos, pos_loc, width)
    steps = [[(i, (i + s) % pos_count) for i in range(pos_count)] for s in range(1, pos_count)]
    remotes = {}
    for video in reversed(range(videos)):
        for which in (2, 1):
            own = qkv[video, which]
            remotes[video, which] = [lax.ppermute(own, "pos", step) for step in steps]
    spatial_gains = [g.reshape(1, head_dim) for g in (spatial_qgain, spatial_kgain)]
    temporal_gains = [g.reshape(1, head_dim) for g in (temporal_qgain, temporal_kgain)]
    results = []
    waiting = []
    blocks = ()
    for video in range(videos):
        weights = score_weights(video, head_dim, qkv, remotes[video, 1], *spatial_gains)
        normed = attend(
            video, head_dim, sub, LARGE if video == videos - 1 else SMALL, weights, qkv, remotes[video, 2], residual,
            spatial_proj, spatial_gate, temporal_scale, temporal_shift,
        )
        if video > 0:
            normed, moved = lax.optimization_barrier((normed, moved))
        moved = exchange(normed, frame_count)
        if video < videos - 1:
            blocks = temporal(video, head_dim, tokens, outer, SMALL, me, moved, temporal_qkv, temporal_gains)
            waiting.append(blocks)
        else:
            if video > 0:
                moved, _ = lax.optimization_barrier((moved, blocks))
            (result,) = temporal(video, head_dim, tokens, 1, TLAST, me, moved, temporal_qkv, temporal_gains)
            results.append(exchange(result, frame_count))
    results = [way_back(blocks, me, outer, inner) for blocks in waiting] + results
    results = [r.reshape(pos_loc, width) for r in results]
    return jnp.stack(results).reshape(videos, frames_loc, pos_loc, width)


def solution(mesh):
    return jax.shard_map(
        per_device,
        mesh=mesh,
        in_specs=(
            P(None, "frame", "pos", None, None),
            P(None, "frame", "pos", None),
            P(),
            P(),
            P(),
            P(),
            P(),
            P(),
            P(),
            P(),
            P(),
        ),
        out_specs=P(None, "frame", "pos", None),
        check_vma=False,
    )
```

```python
import functools
import math

import jax
import jax.numpy as jnp
from jax import lax
from jax.experimental import pallas as pl
from jax.experimental.pallas import tpu as pltpu
from jax.sharding import PartitionSpec as P

EPSILON = 1e-06
LANES = 128
F32 = jnp.float32
BF16 = jnp.bfloat16
TEMPORAL_LIMIT = 50 * 2**20
VMEM_LIMIT = 24 * 2**20
TLAST = 5 * 10**8
PLACE = 7 * 10**9
PICK_LIMIT = 8 * 2**20
SPLITS = 2
SHUFFLE_LIMIT = 8 * 2**20
SMALL, LARGE = 5 * 10**8, 2 * 10**10


def segment_masks(width, head_dim):
    feature = lax.broadcasted_iota(jnp.int32, (width, LANES), 0)
    head = lax.broadcasted_iota(jnp.int32, (width, LANES), 1)
    inside = feature - head * head_dim
    gather = jnp.where((inside >= 0) & (inside < head_dim), 1.0, 0.0).astype(BF16)
    feature = lax.broadcasted_iota(jnp.int32, (LANES, width), 1)
    head = lax.broadcasted_iota(jnp.int32, (LANES, width), 0)
    inside = feature - head * head_dim
    spread = jnp.where((inside >= 0) & (inside < head_dim), 1.0, 0.0).astype(BF16)
    return gather, spread


def split_dot(values, matrix):
    high = values.astype(BF16)
    low = (values - high.astype(F32)).astype(BF16)
    return jnp.dot(high, matrix, preferred_element_type=F32) + jnp.dot(
        low, matrix, preferred_element_type=F32
    )


def head_norm(values, gain_ref, gather, spread, head_dim):
    gain_row = jnp.concatenate([gain_ref[...]] * (values.shape[1] // head_dim), axis=1)
    widened = values.astype(F32)
    squares = split_dot(widened * widened, gather)
    factor = lax.rsqrt(squares * (1.0 / head_dim) + EPSILON)
    return (widened * split_dot(factor, spread) * gain_row).astype(BF16)


def head_window(head, head_dim, width):
    tiles = width // LANES
    start = LANES * min(head * head_dim // LANES, max(tiles - 2, 0))
    span = min(2 * LANES, width)
    lane = lax.broadcasted_iota(jnp.int32, (1, span), 1) + start
    mask = (lane >= head * head_dim) & (lane < (head + 1) * head_dim)
    return start, span, mask


def softmax_rows(scores, scale):
    top = jnp.max(scores, axis=-1, keepdims=True)
    expons = jnp.exp2((scores - top) * scale)
    total = jnp.sum(expons, axis=-1, keepdims=True)
    return (expons * (1.0 / total)).astype(BF16)


def score_kernel(head_dim, video, remotes, *refs):
    qkv_ref = refs[0]
    remote_refs = refs[1 : 1 + remotes]
    query_gain, key_gain, out_ref, query, keys = refs[1 + remotes :]
    pos_loc, width = query.shape
    scale = math.log2(math.e) / math.sqrt(head_dim)
    gather, spread = segment_masks(width, head_dim)
    query[...] = head_norm(qkv_ref[video, 0], query_gain, gather, spread, head_dim)
    keys[0:pos_loc, :] = head_norm(qkv_ref[video, 1], key_gain, gather, spread, head_dim)
    for j, remote in enumerate(remote_refs):
        place = slice((j + 1) * pos_loc, (j + 2) * pos_loc)
        keys[place, :] = head_norm(remote[...], key_gain, gather, spread, head_dim)
    for head in range(width // head_dim):
        start, span, mask = head_window(head, head_dim, width)
        window = slice(start, start + span)
        own = jnp.where(mask, query[:, window], jnp.zeros((), BF16))
        scores = lax.dot_general(
            own, keys[:, window], (((1,), (1,)), ((), ())), preferred_element_type=F32
        )
        out_ref[head] = softmax_rows(scores, scale)


def in_vmem(count):
    return [pl.BlockSpec(memory_space=pltpu.VMEM)] * count


def score_weights(video, head_dim, qkv, remote_keys, query_gain, key_gain):
    _, _, pos_loc, width = qkv.shape
    all_pos = pos_loc * (1 + len(remote_keys))
    heads = width // head_dim
    return pl.pallas_call(
        functools.partial(score_kernel, head_dim, video, len(remote_keys)),
        out_shape=jax.ShapeDtypeStruct((heads, pos_loc, all_pos), BF16),
        in_specs=in_vmem(3 + len(remote_keys)),
        out_specs=pl.BlockSpec(memory_space=pltpu.VMEM),
        scratch_shapes=[pltpu.VMEM((pos_loc, width), BF16), pltpu.VMEM((all_pos, width), BF16)],
        compiler_params=pltpu.CompilerParams(vmem_limit_bytes=VMEM_LIMIT),
        cost_estimate=pl.CostEstimate(flops=SMALL, bytes_accessed=2**20, transcendentals=0),
        name=f"scores_{video}",
    )(qkv, *remote_keys, query_gain, key_gain)


def attend_kernel(head_dim, video, remotes, sub, *refs):
    weights_ref, qkv_ref = refs[:2]
    remote_refs = refs[2 : 2 + remotes]
    residual_ref, proj_ref, gate_ref, scale_ref, shift_ref, out_ref, values, attended = refs[2 + remotes :]
    pos_loc, width = attended.shape
    row = slice(video, video + 1)
    values[0:pos_loc, :] = qkv_ref[video, 2]
    for j, remote in enumerate(remote_refs):
        values[(j + 1) * pos_loc : (j + 2) * pos_loc, :] = remote[...]
    for head in range(width // head_dim):
        start, span, mask = head_window(head, head_dim, width)
        window = slice(start, start + span)
        part = jnp.dot(weights_ref[head], values[:, window], preferred_element_type=F32)
        attended[:, window] = jnp.where(mask, part, attended[:, window])
    mixed = jnp.dot(attended[...].astype(BF16), proj_ref[...], preferred_element_type=F32)
    updated = (residual_ref[video].astype(F32) + gate_ref[row, :] * mixed).astype(BF16)
    widened = updated.astype(F32)
    centred = widened - jnp.mean(widened, axis=-1, keepdims=True)
    spread_of = jnp.mean(centred * centred, axis=-1, keepdims=True)
    scaled = centred * lax.rsqrt(spread_of + EPSILON) * (1.0 + scale_ref[row, :])
    attended[...] = scaled + shift_ref[row, :]
    for i in range(pos_loc // sub):
        out_ref[i] = attended[i * sub : (i + 1) * sub, :].astype(BF16)


def attend(video, head_dim, sub, cost, weights, qkv, remote_values, residual, proj, gate, scale, shift):
    _, _, pos_loc, width = qkv.shape
    all_pos = pos_loc * (1 + len(remote_values))
    return pl.pallas_call(
        functools.partial(attend_kernel, head_dim, video, len(remote_values), sub),
        out_shape=jax.ShapeDtypeStruct((pos_loc // sub, sub, width), BF16),
        in_specs=in_vmem(7 + len(remote_values)),
        out_specs=pl.BlockSpec(memory_space=pltpu.VMEM),
        scratch_shapes=[pltpu.VMEM((all_pos, width), BF16), pltpu.VMEM((pos_loc, width), F32)],
        compiler_params=pltpu.CompilerParams(vmem_limit_bytes=VMEM_LIMIT),
        cost_estimate=pl.CostEstimate(flops=cost, bytes_accessed=2**20, transcendentals=0),
        name=f"attend_{video}",
    )(weights, qkv, *remote_values, residual, proj, gate, scale, shift)


def temporal_kernel(head_dim, tokens, outer, *refs):
    me_ref, in_ref, weight_ref, query_gain, key_gain = refs[:5]
    arranged, query, keys, values, bias, held, arrived = refs[-7:]
    out_refs = refs[5:-7]
    pieces, sub, width = in_ref.shape
    columns = [slice(i * width, (i + 1) * width) for i in range(3)]
    depth = width // SPLITS
    copies = [
        pltpu.make_async_copy(
            weight_ref.at[j * depth : (j + 1) * depth, c],
            held.at[j * depth : (j + 1) * depth, c],
            arrived.at[i, j],
        )
        for i, c in enumerate(columns)
        for j in range(SPLITS)
    ]
    for copy in copies:
        copy.start()
    rows = pieces * sub
    scale = math.log2(math.e) / math.sqrt(head_dim)
    gather, spread = segment_masks(width, head_dim)
    for i in range(pieces):
        arranged[i * sub : (i + 1) * sub, :] = in_ref[i].astype(F32)
    incoming = arranged[...].astype(BF16)
    for i, (place, gain) in enumerate(((query, query_gain), (keys, key_gain), (values, None))):
        for copy in copies[i * SPLITS : (i + 1) * SPLITS]:
            copy.wait()
        projected = jnp.dot(incoming, held[:, columns[i]], preferred_element_type=F32).astype(BF16)
        if gain is not None:
            projected = head_norm(projected, gain, gather, spread, head_dim)
        place[...] = projected
    first = lax.broadcasted_iota(jnp.int32, (rows, rows), 0)
    second = lax.broadcasted_iota(jnp.int32, (rows, rows), 1)
    same = lax.rem(first, tokens) == lax.rem(second, tokens)
    bias[...] = jnp.where(same, 0.0, -1e30)
    for head in range(width // head_dim):
        start, span, mask = head_window(head, head_dim, width)
        window = slice(start, start + span)
        own = jnp.where(mask, query[:, window], jnp.zeros((), BF16))
        scores = lax.dot_general(
            own, keys[:, window], (((1,), (1,)), ((), ())), preferred_element_type=F32
        )
        weights = softmax_rows(scores + bias[...], scale)
        part = jnp.dot(weights, values[:, window], preferred_element_type=F32)
        arranged[:, window] = jnp.where(mask, part, arranged[:, window])
    if outer == 1:
        for i in range(pieces):
            out_refs[0][i] = arranged[i * sub : (i + 1) * sub, :].astype(BF16)
        return
    share = rows // outer
    me = lax.div(me_ref[0], rows // tokens // outer)
    for s in range(outer):
        block = arranged[pl.ds(pl.multiple_of(send_to(me, s, outer) * share, sub), share), :]
        for i in range(share // sub):
            out_refs[s][i] = block[i * sub : (i + 1) * sub, :].astype(BF16)


def temporal(video, head_dim, tokens, outer, cost, me, moved, weight, gains):
    pieces, sub, width = moved.shape
    rows = pieces * sub
    return pl.pallas_call(
        functools.partial(temporal_kernel, head_dim, tokens, outer),
        out_shape=[jax.ShapeDtypeStruct((pieces // outer, sub, width), BF16)] * outer,
        in_specs=[pl.BlockSpec(memory_space=pltpu.SMEM)]
        + in_vmem(1)
        + [pl.BlockSpec(memory_space=pltpu.HBM)]
        + in_vmem(2),
        out_specs=in_vmem(outer),
        scratch_shapes=[pltpu.VMEM((rows, width), F32)]
        + [pltpu.VMEM((rows, width), BF16)] * 3
        + [
            pltpu.VMEM((rows, rows), F32),
            pltpu.VMEM((width, 3 * width), BF16),
            pltpu.SemaphoreType.DMA((3, SPLITS)),
        ],
        compiler_params=pltpu.CompilerParams(vmem_limit_bytes=TEMPORAL_LIMIT),
        cost_estimate=pl.CostEstimate(flops=cost, bytes_accessed=2**20, transcendentals=0),
        name=f"temporal_{video}",
    )(me, moved, weight, *gains)


def send_to(me, step, count):
    return me ^ step if count & (count - 1) == 0 else lax.rem(me + step, count)


def come_from(me, step, count):
    return me ^ step if count & (count - 1) == 0 else lax.rem(me + count - step, count)


def partners(step, count):
    return [i ^ step if count & (count - 1) == 0 else (i + step) % count for i in range(count)]


def regroup_kernel(outer, inner, me_ref, *refs):
    share = refs[0].shape[0] // inner
    me = lax.rem(me_ref[0], inner)
    for t in range(inner):
        to = send_to(me, t, inner)
        for s in range(outer):
            refs[outer + t][s * share : (s + 1) * share] = refs[s][pl.ds(to * share, share)]


def place_kernel(outer, inner, me_ref, *refs):
    share = refs[0].shape[0] // outer
    me = me_ref[0]
    for t in range(inner):
        low = come_from(lax.rem(me, inner), t, inner)
        for s in range(outer):
            high = come_from(lax.div(me, inner), s, outer)
            refs[inner][pl.ds((high * inner + low) * share, share)] = refs[t][
                s * share : (s + 1) * share
            ]


def shuffle(kernel, name, cost, outer, inner, me, arrays, shapes):
    return pl.pallas_call(
        functools.partial(kernel, outer, inner),
        out_shape=[jax.ShapeDtypeStruct(shape, BF16) for shape in shapes],
        in_specs=[pl.BlockSpec(memory_space=pltpu.SMEM)] + in_vmem(len(arrays)),
        out_specs=in_vmem(len(shapes)),
        compiler_params=pltpu.CompilerParams(vmem_limit_bytes=SHUFFLE_LIMIT),
        cost_estimate=pl.CostEstimate(flops=cost, bytes_accessed=2**20, transcendentals=0),
        name=name,
    )(me, *arrays)


def way_back(blocks, me, outer, inner):
    pieces, sub, width = blocks[0].shape
    count = outer * inner
    held = [blocks[0]]
    for s in range(1, outer):
        to = partners(s, outer)
        pairs = [(i, to[i // inner] * inner + i % inner) for i in range(count)]
        held.append(lax.ppermute(blocks[s], "frame", pairs))
    share = pieces // inner
    grouped = shuffle(
        regroup_kernel, "regroup", 1000, outer, inner, me, held, [(outer * share, sub, width)] * inner
    )
    held = [grouped[0]]
    for t in range(1, inner):
        to = partners(t, inner)
        pairs = [(i, i // inner * inner + to[i % inner]) for i in range(count)]
        held.append(lax.ppermute(grouped[t], "frame", pairs))
    (placed,) = shuffle(
        place_kernel, "place", PLACE, outer, inner, me, held, [(count * share, sub, width)]
    )
    return placed


def pick_kernel(video, which, in_ref, out_ref, done):
    copy = pltpu.make_async_copy(in_ref.at[video, which], out_ref, done)
    copy.start()
    copy.wait()


def pick(qkv, video, which):
    return pl.pallas_call(
        functools.partial(pick_kernel, video, which),
        out_shape=jax.ShapeDtypeStruct(qkv.shape[2:], BF16),
        in_specs=[pl.BlockSpec(memory_space=pltpu.HBM)],
        out_specs=pl.BlockSpec(memory_space=pltpu.VMEM),
        scratch_shapes=[pltpu.SemaphoreType.DMA],
        compiler_params=pltpu.CompilerParams(vmem_limit_bytes=PICK_LIMIT),
        cost_estimate=pl.CostEstimate(flops=1000, bytes_accessed=2**20, transcendentals=0),
        name=f"pick_{video}_{which}",
    )(qkv)


def exchange(blocks, frame_count):
    pieces, sub, width = blocks.shape
    split = blocks.reshape(frame_count, pieces // frame_count, sub, width)
    moved = lax.all_to_all(split, "frame", split_axis=0, concat_axis=0, tiled=True)
    return moved.reshape(pieces, sub, width)


def per_device(
    spatial_qkv,
    residual,
    spatial_gate,
    spatial_proj,
    spatial_qgain,
    spatial_kgain,
    temporal_shift,
    temporal_scale,
    temporal_qkv,
    temporal_qgain,
    temporal_kgain,
):
    videos, frames_loc, pos_loc, _, width = spatial_qkv.shape
    head_dim = spatial_qgain.shape[0]
    pos_count = lax.axis_size("pos")
    frame_count = lax.axis_size("frame")
    assert frames_loc == 1
    tokens = pos_loc // frame_count
    sub = math.gcd(tokens, 8)
    inner = math.gcd(frame_count, 4)
    outer = frame_count // inner
    me = lax.axis_index("frame").astype(jnp.int32).reshape(1)
    qkv = jnp.transpose(spatial_qkv.reshape(videos, pos_loc, 3, width), (0, 2, 1, 3))
    residual = residual.reshape(videos, pos_loc, width)
    steps = [[(i, (i + s) % pos_count) for i in range(pos_count)] for s in range(1, pos_count)]
    remotes = {}
    for video in reversed(range(videos)):
        for which in (2, 1):
            own = pick(qkv, video, which)
            remotes[video, which] = [lax.ppermute(own, "pos", step) for step in steps]
    spatial_gains = [g.reshape(1, head_dim) for g in (spatial_qgain, spatial_kgain)]
    temporal_gains = [g.reshape(1, head_dim) for g in (temporal_qgain, temporal_kgain)]
    results = []
    waiting = []
    blocks = ()
    for video in range(videos):
        weights = score_weights(video, head_dim, qkv, remotes[video, 1], *spatial_gains)
        normed = attend(
            video, head_dim, sub, LARGE if video == videos - 1 else SMALL, weights, qkv, remotes[video, 2], residual,
            spatial_proj, spatial_gate, temporal_scale, temporal_shift,
        )
        if video > 0:
            normed, moved = lax.optimization_barrier((normed, moved))
        moved = exchange(normed, frame_count)
        if video < videos - 1:
            blocks = temporal(video, head_dim, tokens, outer, SMALL, me, moved, temporal_qkv, temporal_gains)
            waiting.append(blocks)
        else:
            if video > 0:
                moved, _ = lax.optimization_barrier((moved, blocks))
            (result,) = temporal(video, head_dim, tokens, 1, TLAST, me, moved, temporal_qkv, temporal_gains)
            results.append(exchange(result, frame_count))
    results = [way_back(blocks, me, outer, inner) for blocks in waiting] + results
    results = [r.reshape(pos_loc, width) for r in results]
    return jnp.stack(results).reshape(videos, frames_loc, pos_loc, width)


def solution(mesh):
    return jax.shard_map(
        per_device,
        mesh=mesh,
        in_specs=(
            P(None, "frame", "pos", None, None),
            P(None, "frame", "pos", None),
            P(),
            P(),
            P(),
            P(),
            P(),
            P(),
            P(),
            P(),
            P(),
        ),
        out_specs=P(None, "frame", "pos", None),
        check_vma=False,
    )
```

```python
import functools
import math

import jax
import jax.numpy as jnp
from jax import lax
from jax.experimental import pallas as pl
from jax.experimental.pallas import tpu as pltpu
from jax.sharding import PartitionSpec as P

EPSILON = 1e-06
LANES = 128
F32 = jnp.float32
BF16 = jnp.bfloat16
TEMPORAL_LIMIT = 50 * 2**20
VMEM_LIMIT = 24 * 2**20
TLAST = 5 * 10**8
PLACE = 7 * 10**9
PICK_LIMIT = 8 * 2**20
SPLITS = 2
SHUFFLE_LIMIT = 8 * 2**20
SMALL, LARGE = 5 * 10**8, 2 * 10**10


def segment_masks(width, head_dim):
    feature = lax.broadcasted_iota(jnp.int32, (width, LANES), 0)
    head = lax.broadcasted_iota(jnp.int32, (width, LANES), 1)
    inside = feature - head * head_dim
    gather = jnp.where((inside >= 0) & (inside < head_dim), 1.0, 0.0).astype(BF16)
    feature = lax.broadcasted_iota(jnp.int32, (2 * LANES, width), 1)
    head = lax.rem(lax.broadcasted_iota(jnp.int32, (2 * LANES, width), 0), LANES)
    inside = feature - head * head_dim
    spread = jnp.where((inside >= 0) & (inside < head_dim), 1.0, 0.0).astype(BF16)
    return gather, spread


def split_dot(values, matrix):
    high = values.astype(BF16)
    low = (values - high.astype(F32)).astype(BF16)
    return jnp.dot(high, matrix, preferred_element_type=F32) + jnp.dot(
        low, matrix, preferred_element_type=F32
    )


def head_norm(values, gain_ref, gather, spread, head_dim):
    gain_row = jnp.concatenate([gain_ref[...]] * (values.shape[1] // head_dim), axis=1)
    widened = values.astype(F32)
    squares = split_dot(widened * widened, gather)
    factor = lax.rsqrt(squares * (1.0 / head_dim) + EPSILON)
    high = factor.astype(BF16)
    pieces = jnp.concatenate([high, (factor - high.astype(F32)).astype(BF16)], axis=1)
    return (widened * jnp.dot(pieces, spread, preferred_element_type=F32) * gain_row).astype(BF16)


def head_window(head, head_dim, width):
    tiles = width // LANES
    start = LANES * min(head * head_dim // LANES, max(tiles - 2, 0))
    span = min(2 * LANES, width)
    lane = lax.broadcasted_iota(jnp.int32, (1, span), 1) + start
    mask = (lane >= head * head_dim) & (lane < (head + 1) * head_dim)
    return start, span, mask


def softmax_rows(scores, scale):
    top = jnp.max(scores, axis=-1, keepdims=True)
    expons = jnp.exp2((scores - top) * scale)
    total = jnp.sum(expons, axis=-1, keepdims=True)
    return (expons * (1.0 / total)).astype(BF16)


def score_kernel(head_dim, video, remotes, *refs):
    qkv_ref = refs[0]
    remote_refs = refs[1 : 1 + remotes]
    query_gain, key_gain, out_ref, query, keys = refs[1 + remotes :]
    pos_loc, width = query.shape
    scale = math.log2(math.e) / math.sqrt(head_dim)
    gather, spread = segment_masks(width, head_dim)
    query[...] = head_norm(qkv_ref[video, 0], query_gain, gather, spread, head_dim)
    keys[0:pos_loc, :] = head_norm(qkv_ref[video, 1], key_gain, gather, spread, head_dim)
    for j, remote in enumerate(remote_refs):
        place = slice((j + 1) * pos_loc, (j + 2) * pos_loc)
        keys[place, :] = head_norm(remote[...], key_gain, gather, spread, head_dim)
    for head in range(width // head_dim):
        start, span, mask = head_window(head, head_dim, width)
        window = slice(start, start + span)
        own = jnp.where(mask, query[:, window], jnp.zeros((), BF16))
        scores = lax.dot_general(
            own, keys[:, window], (((1,), (1,)), ((), ())), preferred_element_type=F32
        )
        out_ref[head] = softmax_rows(scores, scale)


def in_vmem(count):
    return [pl.BlockSpec(memory_space=pltpu.VMEM)] * count


def score_weights(video, head_dim, qkv, remote_keys, query_gain, key_gain):
    _, _, pos_loc, width = qkv.shape
    all_pos = pos_loc * (1 + len(remote_keys))
    heads = width // head_dim
    return pl.pallas_call(
        functools.partial(score_kernel, head_dim, video, len(remote_keys)),
        out_shape=jax.ShapeDtypeStruct((heads, pos_loc, all_pos), BF16),
        in_specs=in_vmem(3 + len(remote_keys)),
        out_specs=pl.BlockSpec(memory_space=pltpu.VMEM),
        scratch_shapes=[pltpu.VMEM((pos_loc, width), BF16), pltpu.VMEM((all_pos, width), BF16)],
        compiler_params=pltpu.CompilerParams(vmem_limit_bytes=VMEM_LIMIT),
        cost_estimate=pl.CostEstimate(flops=SMALL, bytes_accessed=2**20, transcendentals=0),
        name=f"scores_{video}",
    )(qkv, *remote_keys, query_gain, key_gain)


def attend_kernel(head_dim, video, remotes, sub, *refs):
    weights_ref, qkv_ref = refs[:2]
    remote_refs = refs[2 : 2 + remotes]
    residual_ref, proj_ref, gate_ref, scale_ref, shift_ref, out_ref, values, attended = refs[2 + remotes :]
    pos_loc, width = attended.shape
    row = slice(video, video + 1)
    values[0:pos_loc, :] = qkv_ref[video, 2]
    for j, remote in enumerate(remote_refs):
        values[(j + 1) * pos_loc : (j + 2) * pos_loc, :] = remote[...]
    for head in range(width // head_dim):
        start, span, mask = head_window(head, head_dim, width)
        window = slice(start, start + span)
        part = jnp.dot(weights_ref[head], values[:, window], preferred_element_type=F32)
        attended[:, window] = jnp.where(mask, part, attended[:, window])
    mixed = jnp.dot(attended[...].astype(BF16), proj_ref[...], preferred_element_type=F32)
    updated = (residual_ref[video].astype(F32) + gate_ref[row, :] * mixed).astype(BF16)
    widened = updated.astype(F32)
    centred = widened - jnp.mean(widened, axis=-1, keepdims=True)
    spread_of = jnp.mean(centred * centred, axis=-1, keepdims=True)
    scaled = centred * lax.rsqrt(spread_of + EPSILON) * (1.0 + scale_ref[row, :])
    attended[...] = scaled + shift_ref[row, :]
    for i in range(pos_loc // sub):
        out_ref[i] = attended[i * sub : (i + 1) * sub, :].astype(BF16)


def attend(video, head_dim, sub, cost, weights, qkv, remote_values, residual, proj, gate, scale, shift):
    _, _, pos_loc, width = qkv.shape
    all_pos = pos_loc * (1 + len(remote_values))
    return pl.pallas_call(
        functools.partial(attend_kernel, head_dim, video, len(remote_values), sub),
        out_shape=jax.ShapeDtypeStruct((pos_loc // sub, sub, width), BF16),
        in_specs=in_vmem(7 + len(remote_values)),
        out_specs=pl.BlockSpec(memory_space=pltpu.VMEM),
        scratch_shapes=[pltpu.VMEM((all_pos, width), BF16), pltpu.VMEM((pos_loc, width), F32)],
        compiler_params=pltpu.CompilerParams(vmem_limit_bytes=VMEM_LIMIT),
        cost_estimate=pl.CostEstimate(flops=cost, bytes_accessed=2**20, transcendentals=0),
        name=f"attend_{video}",
    )(weights, qkv, *remote_values, residual, proj, gate, scale, shift)


def temporal_kernel(head_dim, tokens, outer, *refs):
    me_ref, in_ref, weight_ref, query_gain, key_gain = refs[:5]
    arranged, query, keys, values, bias, held, arrived = refs[-7:]
    out_refs = refs[5:-7]
    pieces, sub, width = in_ref.shape
    columns = [slice(i * width, (i + 1) * width) for i in range(3)]
    depth = width // SPLITS
    copies = [
        pltpu.make_async_copy(
            weight_ref.at[j * depth : (j + 1) * depth, c],
            held.at[j * depth : (j + 1) * depth, c],
            arrived.at[i, j],
        )
        for i, c in enumerate(columns)
        for j in range(SPLITS)
    ]
    for copy in copies:
        copy.start()
    rows = pieces * sub
    scale = math.log2(math.e) / math.sqrt(head_dim)
    gather, spread = segment_masks(width, head_dim)
    for i in range(pieces):
        arranged[i * sub : (i + 1) * sub, :] = in_ref[i].astype(F32)
    incoming = arranged[...].astype(BF16)
    for i, (place, gain) in enumerate(((query, query_gain), (keys, key_gain), (values, None))):
        for copy in copies[i * SPLITS : (i + 1) * SPLITS]:
            copy.wait()
        projected = jnp.dot(incoming, held[:, columns[i]], preferred_element_type=F32).astype(BF16)
        if gain is not None:
            projected = head_norm(projected, gain, gather, spread, head_dim)
        place[...] = projected
    first = lax.broadcasted_iota(jnp.int32, (rows, rows), 0)
    second = lax.broadcasted_iota(jnp.int32, (rows, rows), 1)
    same = lax.rem(first, tokens) == lax.rem(second, tokens)
    bias[...] = jnp.where(same, 0.0, -1e30)
    for head in range(width // head_dim):
        start, span, mask = head_window(head, head_dim, width)
        window = slice(start, start + span)
        own = jnp.where(mask, query[:, window], jnp.zeros((), BF16))
        scores = lax.dot_general(
            own, keys[:, window], (((1,), (1,)), ((), ())), preferred_element_type=F32
        )
        weights = softmax_rows(scores + bias[...], scale)
        part = jnp.dot(weights, values[:, window], preferred_element_type=F32)
        arranged[:, window] = jnp.where(mask, part, arranged[:, window])
    if outer == 1:
        for i in range(pieces):
            out_refs[0][i] = arranged[i * sub : (i + 1) * sub, :].astype(BF16)
        return
    share = rows // outer
    me = lax.div(me_ref[0], rows // tokens // outer)
    for s in range(outer):
        block = arranged[pl.ds(pl.multiple_of(send_to(me, s, outer) * share, sub), share), :]
        for i in range(share // sub):
            out_refs[s][i] = block[i * sub : (i + 1) * sub, :].astype(BF16)


def temporal(video, head_dim, tokens, outer, cost, me, moved, weight, gains):
    pieces, sub, width = moved.shape
    rows = pieces * sub
    return pl.pallas_call(
        functools.partial(temporal_kernel, head_dim, tokens, outer),
        out_shape=[jax.ShapeDtypeStruct((pieces // outer, sub, width), BF16)] * outer,
        in_specs=[pl.BlockSpec(memory_space=pltpu.SMEM)]
        + in_vmem(1)
        + [pl.BlockSpec(memory_space=pltpu.HBM)]
        + in_vmem(2),
        out_specs=in_vmem(outer),
        scratch_shapes=[pltpu.VMEM((rows, width), F32)]
        + [pltpu.VMEM((rows, width), BF16)] * 3
        + [
            pltpu.VMEM((rows, rows), F32),
            pltpu.VMEM((width, 3 * width), BF16),
            pltpu.SemaphoreType.DMA((3, SPLITS)),
        ],
        compiler_params=pltpu.CompilerParams(vmem_limit_bytes=TEMPORAL_LIMIT),
        cost_estimate=pl.CostEstimate(flops=cost, bytes_accessed=2**20, transcendentals=0),
        name=f"temporal_{video}",
    )(me, moved, weight, *gains)


def send_to(me, step, count):
    return me ^ step if count & (count - 1) == 0 else lax.rem(me + step, count)


def come_from(me, step, count):
    return me ^ step if count & (count - 1) == 0 else lax.rem(me + count - step, count)


def partners(step, count):
    return [i ^ step if count & (count - 1) == 0 else (i + step) % count for i in range(count)]


def regroup_kernel(outer, inner, me_ref, *refs):
    share = refs[0].shape[0] // inner
    me = lax.rem(me_ref[0], inner)
    for t in range(inner):
        to = send_to(me, t, inner)
        for s in range(outer):
            refs[outer + t][s * share : (s + 1) * share] = refs[s][pl.ds(to * share, share)]


def place_kernel(outer, inner, me_ref, *refs):
    share = refs[0].shape[0] // outer
    me = me_ref[0]
    for t in range(inner):
        low = come_from(lax.rem(me, inner), t, inner)
        for s in range(outer):
            high = come_from(lax.div(me, inner), s, outer)
            refs[inner][pl.ds((high * inner + low) * share, share)] = refs[t][
                s * share : (s + 1) * share
            ]


def shuffle(kernel, name, cost, outer, inner, me, arrays, shapes):
    return pl.pallas_call(
        functools.partial(kernel, outer, inner),
        out_shape=[jax.ShapeDtypeStruct(shape, BF16) for shape in shapes],
        in_specs=[pl.BlockSpec(memory_space=pltpu.SMEM)] + in_vmem(len(arrays)),
        out_specs=in_vmem(len(shapes)),
        compiler_params=pltpu.CompilerParams(vmem_limit_bytes=SHUFFLE_LIMIT),
        cost_estimate=pl.CostEstimate(flops=cost, bytes_accessed=2**20, transcendentals=0),
        name=name,
    )(me, *arrays)


def way_back(blocks, me, outer, inner):
    pieces, sub, width = blocks[0].shape
    count = outer * inner
    held = [blocks[0]]
    for s in range(1, outer):
        to = partners(s, outer)
        pairs = [(i, to[i // inner] * inner + i % inner) for i in range(count)]
        held.append(lax.ppermute(blocks[s], "frame", pairs))
    share = pieces // inner
    grouped = shuffle(
        regroup_kernel, "regroup", 1000, outer, inner, me, held, [(outer * share, sub, width)] * inner
    )
    held = [grouped[0]]
    for t in range(1, inner):
        to = partners(t, inner)
        pairs = [(i, i // inner * inner + to[i % inner]) for i in range(count)]
        held.append(lax.ppermute(grouped[t], "frame", pairs))
    (placed,) = shuffle(
        place_kernel, "place", PLACE, outer, inner, me, held, [(count * share, sub, width)]
    )
    return placed


def pick_kernel(video, which, in_ref, out_ref, done):
    copy = pltpu.make_async_copy(in_ref.at[video, which], out_ref, done)
    copy.start()
    copy.wait()


def pick(qkv, video, which):
    return pl.pallas_call(
        functools.partial(pick_kernel, video, which),
        out_shape=jax.ShapeDtypeStruct(qkv.shape[2:], BF16),
        in_specs=[pl.BlockSpec(memory_space=pltpu.HBM)],
        out_specs=pl.BlockSpec(memory_space=pltpu.VMEM),
        scratch_shapes=[pltpu.SemaphoreType.DMA],
        compiler_params=pltpu.CompilerParams(vmem_limit_bytes=PICK_LIMIT),
        cost_estimate=pl.CostEstimate(flops=1000, bytes_accessed=2**20, transcendentals=0),
        name=f"pick_{video}_{which}",
    )(qkv)


def exchange(blocks, frame_count):
    pieces, sub, width = blocks.shape
    split = blocks.reshape(frame_count, pieces // frame_count, sub, width)
    moved = lax.all_to_all(split, "frame", split_axis=0, concat_axis=0, tiled=True)
    return moved.reshape(pieces, sub, width)


def per_device(
    spatial_qkv,
    residual,
    spatial_gate,
    spatial_proj,
    spatial_qgain,
    spatial_kgain,
    temporal_shift,
    temporal_scale,
    temporal_qkv,
    temporal_qgain,
    temporal_kgain,
):
    videos, frames_loc, pos_loc, _, width = spatial_qkv.shape
    head_dim = spatial_qgain.shape[0]
    pos_count = lax.axis_size("pos")
    frame_count = lax.axis_size("frame")
    assert frames_loc == 1
    tokens = pos_loc // frame_count
    sub = math.gcd(tokens, 8)
    inner = math.gcd(frame_count, 4)
    outer = frame_count // inner
    me = lax.axis_index("frame").astype(jnp.int32).reshape(1)
    qkv = jnp.transpose(spatial_qkv.reshape(videos, pos_loc, 3, width), (0, 2, 1, 3))
    residual = residual.reshape(videos, pos_loc, width)
    steps = [[(i, (i + s) % pos_count) for i in range(pos_count)] for s in range(1, pos_count)]
    remotes = {}
    for video in reversed(range(videos)):
        for which in (2, 1):
            own = pick(qkv, video, which)
            remotes[video, which] = [lax.ppermute(own, "pos", step) for step in steps]
    spatial_gains = [g.reshape(1, head_dim) for g in (spatial_qgain, spatial_kgain)]
    temporal_gains = [g.reshape(1, head_dim) for g in (temporal_qgain, temporal_kgain)]
    results = []
    waiting = []
    blocks = ()
    for video in range(videos):
        weights = score_weights(video, head_dim, qkv, remotes[video, 1], *spatial_gains)
        normed = attend(
            video, head_dim, sub, LARGE if video == videos - 1 else SMALL, weights, qkv, remotes[video, 2], residual,
            spatial_proj, spatial_gate, temporal_scale, temporal_shift,
        )
        if video > 0:
            normed, moved = lax.optimization_barrier((normed, moved))
        moved = exchange(normed, frame_count)
        if video < videos - 1:
            blocks = temporal(video, head_dim, tokens, outer, SMALL, me, moved, temporal_qkv, temporal_gains)
            waiting.append(blocks)
        else:
            if video > 0:
                moved, _ = lax.optimization_barrier((moved, blocks))
            (result,) = temporal(video, head_dim, tokens, 1, TLAST, me, moved, temporal_qkv, temporal_gains)
            results.append(exchange(result, frame_count))
    results = [way_back(blocks, me, outer, inner) for blocks in waiting] + results
    results = [r.reshape(pos_loc, width) for r in results]
    return jnp.stack(results).reshape(videos, frames_loc, pos_loc, width)


def solution(mesh):
    return jax.shard_map(
        per_device,
        mesh=mesh,
        in_specs=(
            P(None, "frame", "pos", None, None),
            P(None, "frame", "pos", None),
            P(),
            P(),
            P(),
            P(),
            P(),
            P(),
            P(),
            P(),
            P(),
        ),
        out_specs=P(None, "frame", "pos", None),
        check_vma=False,
    )
```

```python
import functools
import math

import jax
import jax.numpy as jnp
from jax import lax
from jax.experimental import pallas as pl
from jax.experimental.pallas import tpu as pltpu
from jax.sharding import PartitionSpec as P

EPSILON = 1e-06
LANES = 128
F32 = jnp.float32
BF16 = jnp.bfloat16
TEMPORAL_LIMIT = 50 * 2**20
VMEM_LIMIT = 24 * 2**20
TLAST = 5 * 10**8
PLACE = 7 * 10**9
PICK_LIMIT = 8 * 2**20
SPLITS = 2
SHUFFLE_LIMIT = 8 * 2**20
SMALL, LARGE = 5 * 10**8, 2 * 10**10


def segment_masks(width, head_dim):
    feature = lax.broadcasted_iota(jnp.int32, (width, LANES), 0)
    head = lax.broadcasted_iota(jnp.int32, (width, LANES), 1)
    inside = feature - head * head_dim
    gather = jnp.where((inside >= 0) & (inside < head_dim), 1.0, 0.0).astype(BF16)
    feature = lax.broadcasted_iota(jnp.int32, (2 * LANES, width), 1)
    head = lax.rem(lax.broadcasted_iota(jnp.int32, (2 * LANES, width), 0), LANES)
    inside = feature - head * head_dim
    spread = jnp.where((inside >= 0) & (inside < head_dim), 1.0, 0.0).astype(BF16)
    return gather, spread


def split_dot(values, matrix):
    high = values.astype(BF16)
    low = (values - high.astype(F32)).astype(BF16)
    return jnp.dot(high, matrix, preferred_element_type=F32) + jnp.dot(
        low, matrix, preferred_element_type=F32
    )


def head_norm(values, gain_ref, gather, spread, head_dim):
    gain_row = jnp.concatenate([gain_ref[...]] * (values.shape[1] // head_dim), axis=1)
    widened = values.astype(F32)
    squares = split_dot(widened * widened, gather)
    factor = lax.rsqrt(squares * (1.0 / head_dim) + EPSILON)
    high = factor.astype(BF16)
    pieces = jnp.concatenate([high, (factor - high.astype(F32)).astype(BF16)], axis=1)
    return (widened * jnp.dot(pieces, spread, preferred_element_type=F32) * gain_row).astype(BF16)


def head_window(head, head_dim, width):
    start = head * head_dim // LANES * LANES
    span = min(-(-(head + 1) * head_dim // LANES) * LANES, width) - start
    lane = lax.broadcasted_iota(jnp.int32, (1, span), 1) + start
    mask = (lane >= head * head_dim) & (lane < (head + 1) * head_dim)
    return start, span, mask


def softmax_rows(scores, scale):
    top = jnp.max(scores, axis=-1, keepdims=True)
    expons = jnp.exp2((scores - top) * scale)
    total = jnp.sum(expons, axis=-1, keepdims=True)
    return (expons * (1.0 / total)).astype(BF16)


def score_kernel(head_dim, video, remotes, *refs):
    qkv_ref = refs[0]
    remote_refs = refs[1 : 1 + remotes]
    query_gain, key_gain, out_ref, query, keys = refs[1 + remotes :]
    pos_loc, width = query.shape
    scale = math.log2(math.e) / math.sqrt(head_dim)
    gather, spread = segment_masks(width, head_dim)
    query[...] = head_norm(qkv_ref[video, 0], query_gain, gather, spread, head_dim)
    keys[0:pos_loc, :] = head_norm(qkv_ref[video, 1], key_gain, gather, spread, head_dim)
    for j, remote in enumerate(remote_refs):
        place = slice((j + 1) * pos_loc, (j + 2) * pos_loc)
        keys[place, :] = head_norm(remote[...], key_gain, gather, spread, head_dim)
    for head in range(width // head_dim):
        start, span, mask = head_window(head, head_dim, width)
        window = slice(start, start + span)
        own = jnp.where(mask, query[:, window], jnp.zeros((), BF16))
        scores = lax.dot_general(
            own, keys[:, window], (((1,), (1,)), ((), ())), preferred_element_type=F32
        )
        out_ref[head] = softmax_rows(scores, scale)


def in_vmem(count):
    return [pl.BlockSpec(memory_space=pltpu.VMEM)] * count


def score_weights(video, head_dim, qkv, remote_keys, query_gain, key_gain):
    _, _, pos_loc, width = qkv.shape
    all_pos = pos_loc * (1 + len(remote_keys))
    heads = width // head_dim
    return pl.pallas_call(
        functools.partial(score_kernel, head_dim, video, len(remote_keys)),
        out_shape=jax.ShapeDtypeStruct((heads, pos_loc, all_pos), BF16),
        in_specs=in_vmem(3 + len(remote_keys)),
        out_specs=pl.BlockSpec(memory_space=pltpu.VMEM),
        scratch_shapes=[pltpu.VMEM((pos_loc, width), BF16), pltpu.VMEM((all_pos, width), BF16)],
        compiler_params=pltpu.CompilerParams(vmem_limit_bytes=VMEM_LIMIT),
        cost_estimate=pl.CostEstimate(flops=SMALL, bytes_accessed=2**20, transcendentals=0),
        name=f"scores_{video}",
    )(qkv, *remote_keys, query_gain, key_gain)


def attend_kernel(head_dim, video, remotes, sub, *refs):
    weights_ref, qkv_ref = refs[:2]
    remote_refs = refs[2 : 2 + remotes]
    residual_ref, proj_ref, gate_ref, scale_ref, shift_ref, out_ref, values, attended = refs[2 + remotes :]
    pos_loc, width = attended.shape
    row = slice(video, video + 1)
    values[0:pos_loc, :] = qkv_ref[video, 2]
    for j, remote in enumerate(remote_refs):
        values[(j + 1) * pos_loc : (j + 2) * pos_loc, :] = remote[...]
    for head in range(width // head_dim):
        start, span, mask = head_window(head, head_dim, width)
        window = slice(start, start + span)
        part = jnp.dot(weights_ref[head], values[:, window], preferred_element_type=F32)
        attended[:, window] = jnp.where(mask, part, attended[:, window])
    mixed = jnp.dot(attended[...].astype(BF16), proj_ref[...], preferred_element_type=F32)
    updated = (residual_ref[video].astype(F32) + gate_ref[row, :] * mixed).astype(BF16)
    widened = updated.astype(F32)
    centred = widened - jnp.mean(widened, axis=-1, keepdims=True)
    spread_of = jnp.mean(centred * centred, axis=-1, keepdims=True)
    scaled = centred * lax.rsqrt(spread_of + EPSILON) * (1.0 + scale_ref[row, :])
    attended[...] = scaled + shift_ref[row, :]
    for i in range(pos_loc // sub):
        out_ref[i] = attended[i * sub : (i + 1) * sub, :].astype(BF16)


def attend(video, head_dim, sub, cost, weights, qkv, remote_values, residual, proj, gate, scale, shift):
    _, _, pos_loc, width = qkv.shape
    all_pos = pos_loc * (1 + len(remote_values))
    return pl.pallas_call(
        functools.partial(attend_kernel, head_dim, video, len(remote_values), sub),
        out_shape=jax.ShapeDtypeStruct((pos_loc // sub, sub, width), BF16),
        in_specs=in_vmem(7 + len(remote_values)),
        out_specs=pl.BlockSpec(memory_space=pltpu.VMEM),
        scratch_shapes=[pltpu.VMEM((all_pos, width), BF16), pltpu.VMEM((pos_loc, width), F32)],
        compiler_params=pltpu.CompilerParams(vmem_limit_bytes=VMEM_LIMIT),
        cost_estimate=pl.CostEstimate(flops=cost, bytes_accessed=2**20, transcendentals=0),
        name=f"attend_{video}",
    )(weights, qkv, *remote_values, residual, proj, gate, scale, shift)


def temporal_kernel(head_dim, tokens, outer, *refs):
    me_ref, in_ref, weight_ref, query_gain, key_gain = refs[:5]
    arranged, query, keys, values, bias, held, arrived = refs[-7:]
    out_refs = refs[5:-7]
    pieces, sub, width = in_ref.shape
    columns = [slice(i * width, (i + 1) * width) for i in range(3)]
    depth = width // SPLITS
    copies = [
        pltpu.make_async_copy(
            weight_ref.at[j * depth : (j + 1) * depth, c],
            held.at[j * depth : (j + 1) * depth, c],
            arrived.at[i, j],
        )
        for i, c in enumerate(columns)
        for j in range(SPLITS)
    ]
    for i, copy in enumerate(copies):
        copy.start(priority=0 if i < SPLITS else 1)
    rows = pieces * sub
    scale = math.log2(math.e) / math.sqrt(head_dim)
    gather, spread = segment_masks(width, head_dim)
    first = lax.broadcasted_iota(jnp.int32, (rows, rows), 0)
    second = lax.broadcasted_iota(jnp.int32, (rows, rows), 1)
    same = lax.rem(first, tokens) == lax.rem(second, tokens)
    bias[...] = jnp.where(same, 0.0, -1e30)
    for i in range(pieces):
        arranged[i * sub : (i + 1) * sub, :] = in_ref[i].astype(F32)
    incoming = arranged[...].astype(BF16)
    for i, (place, gain) in enumerate(((query, query_gain), (keys, key_gain), (values, None))):
        for copy in copies[i * SPLITS : (i + 1) * SPLITS]:
            copy.wait()
        projected = jnp.dot(incoming, held[:, columns[i]], preferred_element_type=F32).astype(BF16)
        if gain is not None:
            projected = head_norm(projected, gain, gather, spread, head_dim)
        place[...] = projected
    for head in range(width // head_dim):
        start, span, mask = head_window(head, head_dim, width)
        window = slice(start, start + span)
        own = jnp.where(mask, query[:, window], jnp.zeros((), BF16))
        scores = lax.dot_general(
            own, keys[:, window], (((1,), (1,)), ((), ())), preferred_element_type=F32
        )
        weights = softmax_rows(scores + bias[...], scale)
        part = jnp.dot(weights, values[:, window], preferred_element_type=F32)
        arranged[:, window] = jnp.where(mask, part, arranged[:, window])
    if outer == 1:
        for i in range(pieces):
            out_refs[0][i] = arranged[i * sub : (i + 1) * sub, :].astype(BF16)
        return
    share = rows // outer
    me = lax.div(me_ref[0], rows // tokens // outer)
    for s in range(outer):
        block = arranged[pl.ds(pl.multiple_of(send_to(me, s, outer) * share, sub), share), :]
        for i in range(share // sub):
            out_refs[s][i] = block[i * sub : (i + 1) * sub, :].astype(BF16)


def temporal(video, head_dim, tokens, outer, cost, me, moved, weight, gains):
    pieces, sub, width = moved.shape
    rows = pieces * sub
    return pl.pallas_call(
        functools.partial(temporal_kernel, head_dim, tokens, outer),
        out_shape=[jax.ShapeDtypeStruct((pieces // outer, sub, width), BF16)] * outer,
        in_specs=[pl.BlockSpec(memory_space=pltpu.SMEM)]
        + in_vmem(1)
        + [pl.BlockSpec(memory_space=pltpu.HBM)]
        + in_vmem(2),
        out_specs=in_vmem(outer),
        scratch_shapes=[pltpu.VMEM((rows, width), F32)]
        + [pltpu.VMEM((rows, width), BF16)] * 3
        + [
            pltpu.VMEM((rows, rows), F32),
            pltpu.VMEM((width, 3 * width), BF16),
            pltpu.SemaphoreType.DMA((3, SPLITS)),
        ],
        compiler_params=pltpu.CompilerParams(vmem_limit_bytes=TEMPORAL_LIMIT),
        cost_estimate=pl.CostEstimate(flops=cost, bytes_accessed=2**20, transcendentals=0),
        name=f"temporal_{video}",
    )(me, moved, weight, *gains)


def send_to(me, step, count):
    return me ^ step if count & (count - 1) == 0 else lax.rem(me + step, count)


def come_from(me, step, count):
    return me ^ step if count & (count - 1) == 0 else lax.rem(me + count - step, count)


def partners(step, count):
    return [i ^ step if count & (count - 1) == 0 else (i + step) % count for i in range(count)]


def regroup_kernel(outer, inner, me_ref, *refs):
    share = refs[0].shape[0] // inner
    me = lax.rem(me_ref[0], inner)
    for t in range(inner):
        to = send_to(me, t, inner)
        for s in range(outer):
            refs[outer + t][s * share : (s + 1) * share] = refs[s][pl.ds(to * share, share)]


def place_kernel(outer, inner, me_ref, *refs):
    share = refs[0].shape[0] // outer
    me = me_ref[0]
    for t in range(inner):
        low = come_from(lax.rem(me, inner), t, inner)
        for s in range(outer):
            high = come_from(lax.div(me, inner), s, outer)
            refs[inner][pl.ds((high * inner + low) * share, share)] = refs[t][
                s * share : (s + 1) * share
            ]


def shuffle(kernel, name, cost, outer, inner, me, arrays, shapes):
    return pl.pallas_call(
        functools.partial(kernel, outer, inner),
        out_shape=[jax.ShapeDtypeStruct(shape, BF16) for shape in shapes],
        in_specs=[pl.BlockSpec(memory_space=pltpu.SMEM)] + in_vmem(len(arrays)),
        out_specs=in_vmem(len(shapes)),
        compiler_params=pltpu.CompilerParams(vmem_limit_bytes=SHUFFLE_LIMIT),
        cost_estimate=pl.CostEstimate(flops=cost, bytes_accessed=2**20, transcendentals=0),
        name=name,
    )(me, *arrays)


def way_back(blocks, me, outer, inner):
    pieces, sub, width = blocks[0].shape
    count = outer * inner
    held = [blocks[0]]
    for s in range(1, outer):
        to = partners(s, outer)
        pairs = [(i, to[i // inner] * inner + i % inner) for i in range(count)]
        held.append(lax.ppermute(blocks[s], "frame", pairs))
    share = pieces // inner
    grouped = shuffle(
        regroup_kernel, "regroup", 1000, outer, inner, me, held, [(outer * share, sub, width)] * inner
    )
    held = [grouped[0]]
    for t in range(1, inner):
        to = partners(t, inner)
        pairs = [(i, i // inner * inner + to[i % inner]) for i in range(count)]
        held.append(lax.ppermute(grouped[t], "frame", pairs))
    (placed,) = shuffle(
        place_kernel, "place", PLACE, outer, inner, me, held, [(count * share, sub, width)]
    )
    return placed


def pick_kernel(video, which, in_ref, out_ref, done):
    copy = pltpu.make_async_copy(in_ref.at[video, which], out_ref, done)
    copy.start()
    copy.wait()


def pick(qkv, video, which):
    return pl.pallas_call(
        functools.partial(pick_kernel, video, which),
        out_shape=jax.ShapeDtypeStruct(qkv.shape[2:], BF16),
        in_specs=[pl.BlockSpec(memory_space=pltpu.HBM)],
        out_specs=pl.BlockSpec(memory_space=pltpu.VMEM),
        scratch_shapes=[pltpu.SemaphoreType.DMA],
        compiler_params=pltpu.CompilerParams(vmem_limit_bytes=PICK_LIMIT),
        cost_estimate=pl.CostEstimate(flops=1000, bytes_accessed=2**20, transcendentals=0),
        name=f"pick_{video}_{which}",
    )(qkv)


def exchange(blocks, frame_count):
    pieces, sub, width = blocks.shape
    split = blocks.reshape(frame_count, pieces // frame_count, sub, width)
    moved = lax.all_to_all(split, "frame", split_axis=0, concat_axis=0, tiled=True)
    return moved.reshape(pieces, sub, width)


def per_device(
    spatial_qkv,
    residual,
    spatial_gate,
    spatial_proj,
    spatial_qgain,
    spatial_kgain,
    temporal_shift,
    temporal_scale,
    temporal_qkv,
    temporal_qgain,
    temporal_kgain,
):
    videos, frames_loc, pos_loc, _, width = spatial_qkv.shape
    head_dim = spatial_qgain.shape[0]
    pos_count = lax.axis_size("pos")
    frame_count = lax.axis_size("frame")
    assert frames_loc == 1
    tokens = pos_loc // frame_count
    sub = math.gcd(tokens, 8)
    inner = math.gcd(frame_count, 4)
    outer = frame_count // inner
    me = lax.axis_index("frame").astype(jnp.int32).reshape(1)
    qkv = jnp.transpose(spatial_qkv.reshape(videos, pos_loc, 3, width), (0, 2, 1, 3))
    residual = residual.reshape(videos, pos_loc, width)
    steps = [[(i, (i + s) % pos_count) for i in range(pos_count)] for s in range(1, pos_count)]
    remotes = {}
    for video in reversed(range(videos)):
        for which in (2, 1):
            own = pick(qkv, video, which)
            remotes[video, which] = [lax.ppermute(own, "pos", step) for step in steps]
    spatial_gains = [g.reshape(1, head_dim) for g in (spatial_qgain, spatial_kgain)]
    temporal_gains = [g.reshape(1, head_dim) for g in (temporal_qgain, temporal_kgain)]
    results = []
    waiting = []
    blocks = ()
    for video in range(videos):
        weights = score_weights(video, head_dim, qkv, remotes[video, 1], *spatial_gains)
        normed = attend(
            video, head_dim, sub, LARGE if video == videos - 1 else SMALL, weights, qkv, remotes[video, 2], residual,
            spatial_proj, spatial_gate, temporal_scale, temporal_shift,
        )
        if video > 0:
            normed, moved = lax.optimization_barrier((normed, moved))
        moved = exchange(normed, frame_count)
        if video < videos - 1:
            blocks = temporal(video, head_dim, tokens, outer, SMALL, me, moved, temporal_qkv, temporal_gains)
            waiting.append(blocks)
        else:
            if video > 0:
                moved, _ = lax.optimization_barrier((moved, blocks))
            (result,) = temporal(video, head_dim, tokens, 1, TLAST, me, moved, temporal_qkv, temporal_gains)
            results.append(exchange(result, frame_count))
    results = [way_back(blocks, me, outer, inner) for blocks in waiting] + results
    results = [r.reshape(pos_loc, width) for r in results]
    return jnp.stack(results).reshape(videos, frames_loc, pos_loc, width)


def solution(mesh):
    return jax.shard_map(
        per_device,
        mesh=mesh,
        in_specs=(
            P(None, "frame", "pos", None, None),
            P(None, "frame", "pos", None),
            P(),
            P(),
            P(),
            P(),
            P(),
            P(),
            P(),
            P(),
            P(),
        ),
        out_specs=P(None, "frame", "pos", None),
        check_vma=False,
    )
```
